512 devices in a mesh: radial: 4 (over x), mode: 128 (over z, y, core).
Axes of the slice: x: 4, y: 4, z: 16, core: 2. Of those that a mesh axis runs over, the one named last changes fastest.
Arguments:
- spectral_state: float32 [256, 3, 8, 2, 513], P('mode', None, 'radial'), may hold values from -6 to 6
- synthesis_table: bfloat16 [256, 513, 512], P('mode', None, 'radial'), may hold values from -0.0078125 to 0.0078125
- low_orders: int32 [256], replicated, may hold values from 0 to 255, each once
- diffusion: float32 [3], replicated, may hold values from 200 to 2000
- coupling: float32 [3], replicated, may hold values from 1 to 4
Outputs:
- updated: float32 [256, 3, 8, 2, 513], P('mode', None, 'radial')
The draws below stay inside these ranges and needn't reach their ends.
Inputs may be any that keep to these rules, and one draw needn't show every extreme that they name: A permutation: pair j holds the orders low_orders[j] and 511 - low_orders[j].
All inputs are finite; a program needn't handle non-finite values.
Results may differ from the reference program's by a relative error of at most 0.0023.
The reference program's roundings to bfloat16 on the way (of `legendre`, `coeffs`, `fourier` and `returned`) count: a program that leaves them out, or rounds other values in their place, can miss the bound.
Values may be sent and summed in bfloat16 or wider, within the bound.
A program may use at most 64 MiB of HBM per device.

```python
import math
import jax
import jax.numpy as jnp
from jax import lax

ORDERS = 512
PAIRS = 256
ROWS = 513
NLAT = 1024
NH = 512
NLON = 1536
SHELLS = 8


def level_of(stream_key, shape, cuts, smallest, top_value):
    def one(axis_at, parts):
        heights = jax.random.uniform(jax.random.fold_in(jax.random.fold_in(stream_key, 6), axis_at), (parts,), jnp.float32, smallest / len(cuts), top_value / len(cuts))
        return jnp.repeat(jnp.exp(heights), shape[axis_at] // parts).reshape((-1,) + (1,) * (len(shape) - axis_at - 1))

    gain = one(*cuts[0])
    for cut in cuts[1:]:
        gain = gain * one(*cut)
    return gain


def scatter_about(own_key, extent, scale, bound, shards=(), kind=jnp.bfloat16):
    loudness = level_of(own_key, extent, shards, -0.22, 0.18) if shards else 1.0
    entries = jax.random.normal(own_key, extent, jnp.float32) * scale * loudness
    return jnp.minimum(jnp.maximum(entries, -bound), bound).astype(kind)


def setup_inputs(seed: int = 0) -> dict:
    splits = jax.random.split(jax.random.key(seed), 6)
    return {
        "spectral_state": scatter_about(splits[0], (PAIRS, 3, SHELLS, 2, ROWS), 1.0, 6.0, ((0, 128), (2, 4)), jnp.float32),
        "synthesis_table": scatter_about(splits[1], (PAIRS, ROWS, NH), (2 * ORDERS * ROWS) ** -0.5, 0.0078125, ((0, 128), (2, 4))),
        "low_orders": jax.random.permutation(splits[2], PAIRS).astype(jnp.int32),
        "diffusion": jnp.clip(jnp.exp(jax.random.uniform(splits[3], (3,), jnp.float32, math.log(200.0), math.log(2000.0))), 200.0, 2000.0),
        "coupling": jnp.clip(jax.random.uniform(splits[4], (3,), jnp.float32, 1.0, 4.0), 1.0, 4.0),
    }


inner_radius = 0.538
shell_step = 1.0 / 2048.0

def pair_layout(low_orders):
    row_index = jnp.arange(ORDERS + 1, dtype=jnp.int32)[None, :]
    lower_col = low_orders.astype(jnp.int32)[:, None]
    in_lower = row_index < ORDERS - lower_col
    degree = jnp.where(in_lower, lower_col + row_index, row_index - 1)
    order_of = jnp.where(in_lower, lower_col, ORDERS - 1 - lower_col)
    return (in_lower, degree, order_of)

def full_table(pair_table, pair_sign):
    northern = pair_table.astype(jnp.float32)
    southern = (northern * pair_sign[:, None])[:, ::-1]
    return jnp.concatenate([northern, southern], axis=1)

def reference(spectral_state, synthesis_table, low_orders, diffusion, coupling):
    in_lower, degree, order_of = pair_layout(low_orders)
    row_sign = jnp.where((degree + order_of) % 2 == 0, 1.0, -1.0).astype(jnp.float32)
    order_mask = jnp.stack([in_lower, jnp.logical_not(in_lower)], axis=1).astype(jnp.float32)
    coeffs = spectral_state.astype(jnp.bfloat16)

    def synth_pair(inputs):
        pair_table, pair_sign, pair_mask, pair_coeffs = inputs
        legendre = full_table(pair_table, pair_sign)
        values = jnp.einsum('rj,fscr,kr->kfscj', legendre, pair_coeffs.astype(jnp.float32), pair_mask, precision=lax.Precision.HIGHEST)
        return values.astype(jnp.bfloat16)
    fourier = lax.map(synth_pair, (synthesis_table, row_sign, order_mask, coeffs))
    by_shell = jnp.transpose(fourier, (3, 2, 5, 0, 1, 4)).astype(jnp.float32)
    lower_orders = low_orders.astype(jnp.int32)
    flat_orders = jnp.stack([lower_orders, ORDERS - 1 - lower_orders], axis=1).reshape(ORDERS)
    analysis_scale = 2.0 * math.sqrt(ORDERS * (ORDERS + 1) / (NLAT * NLON))

    def transform_shell(values):
        values = values.reshape(3, NLAT, ORDERS, 2)
        real_part = jnp.zeros((3, NLAT, ORDERS + 1), jnp.float32).at[:, :, flat_orders].set(values[..., 0])
        imag_part = jnp.zeros((3, NLAT, ORDERS + 1), jnp.float32).at[:, :, flat_orders].set(values[..., 1])
        grid_values = NLON * jnp.fft.irfft(lax.complex(real_part, imag_part), n=NLON, axis=-1)
        products = jnp.stack([grid_values[0] * grid_values[1], grid_values[0] * grid_values[2], grid_values[1] * grid_values[2]])
        spectrum = jnp.fft.rfft(products, axis=-1)[:, :, flat_orders]
        result = jnp.stack([jnp.real(spectrum), jnp.imag(spectrum)], axis=-1) * analysis_scale
        return result.reshape(3, NLAT, PAIRS, 2, 2).astype(jnp.bfloat16)
    returned = lax.map(transform_shell, by_shell)
    returned = jnp.transpose(returned, (3, 4, 1, 0, 5, 2))

    def analyse_pair(inputs):
        pair_table, pair_sign, pair_mask, pair_back = inputs
        legendre = full_table(pair_table, pair_sign)
        return jnp.einsum('rj,kfscj,kr->fscr', legendre, pair_back.astype(jnp.float32), pair_mask, precision=lax.Precision.HIGHEST)
    nonlinear = lax.map(analyse_pair, (synthesis_table, row_sign, order_mask, returned))
    degree_term = degree.astype(jnp.float32)
    radius = inner_radius + (jnp.arange(SHELLS, dtype=jnp.float32) + 0.5) * shell_step
    damping = (degree_term * (degree_term + 1.0))[:, None, None, None, :] * (shell_step * shell_step) / (radius * radius)[None, None, :, None, None]
    rate_full = diffusion.reshape(1, 3, 1, 1, 1)
    strength = coupling.reshape(1, 3, 1, 1, 1)
    padded = jnp.pad(spectral_state, ((0, 0), (0, 0), (1, 1), (0, 0), (0, 0)))
    laplace = padded[:, :, 2:] - 2.0 * spectral_state + padded[:, :, :-2] - damping * spectral_state
    drive = spectral_state + rate_full * (laplace + strength * nonlinear)
    diagonal = jnp.broadcast_to(1.0 + rate_full * (2.0 + damping), drive.shape)
    drive_by = jnp.moveaxis(drive, 2, 0)
    diagonal_by = jnp.moveaxis(diagonal, 2, 0)
    rate_col = diffusion.reshape(1, 3, 1, 1)
    blank_state = jnp.zeros(drive_by.shape[1:], jnp.float32)

    def forward(running, inputs):
        pivot, solved = running
        diag_now, drive_now = inputs
        denom_now = diag_now + rate_col * pivot
        pivot_new = -rate_col / denom_now
        solved_new = (drive_now + rate_col * solved) / denom_now
        return ((pivot_new, solved_new), (pivot_new, solved_new))
    _, (pivots, solveds) = lax.scan(forward, (blank_state, blank_state), (diagonal_by, drive_by))

    def backward(next_value, inputs):
        pivot, solved = inputs
        value = solved - pivot * next_value
        return (value, value)
    _, updated_by = lax.scan(backward, blank_state, (pivots, solveds), reverse=True)
    return jnp.moveaxis(updated_by, 0, 2)
```

```python
import math

import jax
import jax.numpy as jnp
import ml_dtypes
import numpy as np
from jax import lax
from jax.experimental import pallas as pl
from jax.experimental.pallas import tpu as pltpu
from jax.sharding import PartitionSpec as P

inner_radius = 0.538
shell_step = 1.0 / 2048.0

ORDERS = 512
HALF = 256
ROWS = 513
PADDED = 640
NLON = 1536
QUARTER = 384
NLAT = 1024
SLABS = 4
NEAR = 8
FAR = 16
KAPPA = 2.0 * math.sqrt(ORDERS * (ORDERS + 1) / (NLAT * NLON))
MESH = pl.DeviceIdType.MESH
F32 = jnp.float32
BF16 = jnp.bfloat16


def wave_tables():
    low = np.arange(HALF)
    even = np.where(low % 2 == 0, low, ORDERS - 1 - low)
    twice = 2 * np.arange(QUARTER)[:, None] + 1
    heads, tails = [], []
    for order in (even, ORDERS - 1 - even):
        weight = np.where(order == 0, 1.0, 2.0)
        angle = (order[None, :] * twice % (2 * NLON)) * (math.pi / NLON)
        for wave in (weight * np.cos(angle), -weight * np.sin(angle)):
            head = wave.astype(ml_dtypes.bfloat16)
            heads.append(head)
            tails.append((wave - head.astype(np.float64)).astype(ml_dtypes.bfloat16))
    return np.stack(heads + tails)


def nn(a, b):
    return lax.dot_general(a, b, (((1,), (0,)), ((), ())), preferred_element_type=F32)


def nt(a, b):
    return lax.dot_general(a, b, (((1,), (1,)), ((), ())), preferred_element_type=F32)


def kernel(
    state, table, low_row, lows, diffusion, coupling, waves, out,
    wave_raw, wave_own, masked, st, cg, flat, s1, s2, r1, r2, s3, r3, s4, r4, mid, mid3, inv, send_x, recv_x, total,
    wave_sem, sem_cs, sem_cr, sem_1s, sem_1r, sem_2s, sem_2r, sem_3s, sem_3r, sem_4s, sem_4r, sem_us, sem_ur,
):
    slab = lax.axis_index("radial")
    mode = lax.axis_index("mode")
    far = mode // NEAR
    near = lax.rem(mode, NEAR)

    barrier = pltpu.get_barrier_semaphore()
    for k in range(1, SLABS):
        pl.semaphore_signal(barrier, inc=1, device_id=(lax.rem(slab + k, SLABS), mode), device_id_type=MESH)
    for k in range(1, NEAR):
        pl.semaphore_signal(barrier, inc=1, device_id=(slab, far * NEAR + lax.rem(near + k, NEAR)), device_id_type=MESH)
    for k in range(1, FAR):
        pl.semaphore_signal(barrier, inc=1, device_id=(slab, lax.rem(far + k, FAR) * NEAR + near), device_id_type=MESH)

    wave_copy = pltpu.make_async_copy(waves, wave_raw, wave_sem)
    wave_copy.start()

    st[...] = jnp.zeros_like(st)
    for f in range(3):
        for s in range(2):
            for c in range(2):
                for p in range(2):
                    row = f * 8 + s * 4 + c * 2 + p
                    st[row : row + 1, 0:ROWS] = state[p, f, s, c : c + 1, :]
    cg[slab] = st[...].astype(BF16)

    pl.semaphore_wait(barrier, SLABS + NEAR + FAR - 3)

    def x_copy(source, target, k, send, recv):
        return pltpu.make_async_remote_copy(
            src_ref=source, dst_ref=target, send_sem=send.at[k - 1], recv_sem=recv.at[k - 1],
            device_id=(lax.rem(slab + k, SLABS), mode), device_id_type=MESH,
        )

    def near_copy(source, target, k, send, recv):
        return pltpu.make_async_remote_copy(
            src_ref=source, dst_ref=target, send_sem=send.at[k - 1], recv_sem=recv.at[k - 1],
            device_id=(slab, far * NEAR + lax.rem(near + k, NEAR)), device_id_type=MESH,
        )

    def far_copy(source, target, k, send, recv):
        return pltpu.make_async_remote_copy(
            src_ref=source, dst_ref=target, send_sem=send.at[k - 1], recv_sem=recv.at[k - 1],
            device_id=(slab, lax.rem(far + k, FAR) * NEAR + near), device_id_type=MESH,
        )

    coefs = [x_copy(cg.at[slab], cg.at[slab], k, sem_cs, sem_cr) for k in range(1, SLABS)]
    for copy in coefs:
        copy.start()

    for p in range(2):
        low = lows[mode * 2 + p]
        low_even = lax.rem(low, 2) == 0
        for start, size in ((0, 512), (512, 128)):
            row = lax.broadcasted_iota(jnp.int32, (size, 128), 0) + start
            if start == 0:
                values = table[p, 0:512, :].astype(F32)
            else:
                last = table[p, 512:513, :].astype(F32)
                values = jnp.where(row == 512, jnp.broadcast_to(last, (128, 128)), 0.0)
            in_lower = row < ORDERS - low
            even_order = in_lower == low_even
            odd_sum = jnp.where(in_lower, lax.rem(row, 2), lax.rem(row + low, 2))
            sign = 1.0 - 2.0 * odd_sum.astype(F32)
            for q in range(2):
                north = jnp.where(even_order == (q == 0), values, 0.0)
                masked[p, start : start + size, q * 128 : (q + 1) * 128] = north.astype(BF16)
                masked[p, start : start + size, (2 + q) * 128 : (3 + q) * 128] = (north * sign).astype(BF16)

    for copy in coefs:
        copy.wait()

    gathered = [cg[i].astype(F32) for i in range(SLABS)]
    lhs = jnp.concatenate(
        [gathered[i][f * 8 : (f + 1) * 8] for f in range(3) for i in range(SLABS)], axis=0
    ).astype(BF16)
    first_pair = lax.rem(lax.broadcasted_iota(jnp.int32, (96, 512), 0), 2) == 0
    synth = jnp.where(first_pair, nn(lhs, masked[0]), nn(lhs, masked[1]))
    for b in range(4):
        flat[b * 96 : (b + 1) * 96, :] = synth[:, b * 128 : (b + 1) * 128]
    for g in range(3):
        block = flat[g * 128 : (g + 1) * 128, :].T
        s1[:, :, g * 128 : (g + 1) * 128] = block.reshape(NEAR, FAR, 128).astype(BF16)
    hop1 = [near_copy(s1.at[lax.rem(near + k, NEAR)], r1.at[near], k, sem_1s, sem_1r) for k in range(1, NEAR)]
    for copy in hop1:
        copy.start()
    r1[near] = s1[near]

    wave_copy.wait()
    pick = (
        lax.broadcasted_iota(jnp.int32, (HALF, HALF), 0) == jnp.broadcast_to(low_row[...], (HALF, HALF))
    ).astype(F32).astype(BF16)
    for q in range(8):
        wave_own[q] = nn(wave_raw[q], pick).astype(BF16)

    for copy in hop1:
        copy.wait()
    arrived = r1[...].reshape(128, QUARTER).astype(F32)
    for g in range(3):
        mid[g] = arrived[:, g * 128 : (g + 1) * 128]
    for z in range(FAR):
        s2[z] = jnp.concatenate([mid[g, pl.ds(z, NEAR, stride=FAR), :] for g in range(3)], axis=0).astype(BF16)
    hop2 = [far_copy(s2.at[lax.rem(far + k, FAR)], r2.at[far], k, sem_2s, sem_2r) for k in range(1, FAR)]
    for copy in hop2:
        copy.start()
    r2[far] = s2[far]

    row8 = lax.broadcasted_iota(jnp.int32, (8, PADDED), 0)
    lane8 = lax.broadcasted_iota(jnp.int32, (8, PADDED), 1)
    low8 = jnp.where(lax.rem(row8, 2) == 0, lows[mode * 2], lows[mode * 2 + 1])
    degree = jnp.where(lane8 < ORDERS - low8, low8 + lane8, lane8 - 1).astype(F32)
    degree = degree * (degree + 1.0) * (shell_step * shell_step)
    first_shell = row8 < 4
    for f in range(3):
        diagonal = []
        for s in range(8):
            radius = inner_radius + (s + 0.5) * shell_step
            diagonal.append(degree * (1.0 / (radius * radius)) + (1.0 / diffusion[f] + 2.0))
        leading = [jnp.ones((8, PADDED), F32), diagonal[0]]
        trailing = [jnp.ones((8, PADDED), F32), diagonal[7]]
        for s in range(1, 8):
            leading.append(diagonal[s] * leading[s] - leading[s - 1])
            trailing.append(diagonal[7 - s] * trailing[s] - trailing[s - 1])
        share = 1.0 / leading[8]
        scaled = [value * share for value in leading]

        def entry(i, j):
            return scaled[min(i, j)] * trailing[7 - max(i, j)]

        for i in range(SLABS):
            for j in range(i, SLABS):
                inv[f, 0, i, j] = jnp.where(first_shell, entry(2 * i, 2 * j), entry(2 * i + 1, 2 * j + 1))
                inv[f, 1, i, j] = jnp.where(first_shell, entry(2 * i, 2 * j + 1), entry(2 * i + 1, 2 * j))
                if i != j:
                    inv[f, 0, j, i] = jnp.where(first_shell, entry(2 * i, 2 * j), entry(2 * i + 1, 2 * j + 1))
                    inv[f, 1, j, i] = jnp.where(first_shell, entry(2 * i + 1, 2 * j), entry(2 * i, 2 * j + 1))

    for copy in hop2:
        copy.wait()
    arrived = r2[...].astype(F32)
    for g in range(3):
        flat[g * 128 : (g + 1) * 128, :] = arrived[:, g * 8 : (g + 1) * 8, :].reshape(128, 128).T

    parts = []
    for q in range(2):
        for c in range(2):
            rows = [
                jnp.concatenate(
                    [flat[pl.ds((h * 2 + q) * 96 + c * 2 + p, 24, stride=4), :] for p in range(2)], axis=1
                )
                for h in range(2)
            ]
            data = jnp.concatenate(rows, axis=0).astype(BF16)
            at = q * 2 + c
            parts.append(nt(data, wave_own[at]) + nt(data, wave_own[4 + at]))
    a, b = parts[0] + parts[2], parts[1] + parts[3]
    c, d = parts[0] - parts[2], parts[1] - parts[3]
    images = (a + b, a - b, c - d, c + d)
    sums = [[], [], [], []]
    for h in range(2):
        for left, right in ((0, 1), (0, 2), (1, 2)):
            u, v = h * 24 + left * 8, h * 24 + right * 8
            p1, p2, p3, p4 = [image[u : u + 8] * image[v : v + 8] for image in images]
            both, across = p1 + p2, p3 + p4
            turn, twist = p1 - p2, p4 - p3
            sums[0].append(both + across)
            sums[1].append(turn + twist)
            sums[2].append(both - across)
            sums[3].append(turn - twist)
    lowest = jnp.broadcast_to(low_row[...], (48, HALF)) == 0
    for q in range(2):
        for c in range(2):
            at = q * 2 + c
            value = jnp.concatenate(sums[at], axis=0)
            head = value.astype(BF16)
            tail = (value - head.astype(F32)).astype(BF16)
            answer = nn(head, wave_own[at]) + (nn(tail, wave_own[at]) + nn(head, wave_own[4 + at]))
            if q == 0:
                answer = answer * jnp.where(lowest, KAPPA, 0.5 * KAPPA)
            else:
                answer = answer * (0.5 * KAPPA)
            for h in range(2):
                for p in range(2):
                    flat[pl.ds((h * 2 + q) * 96 + c * 2 + p, 24, stride=4), :] = answer[
                        h * 24 : (h + 1) * 24, p * 128 : (p + 1) * 128
                    ]
    turned = [flat[g * 128 : (g + 1) * 128, :].T.reshape(FAR, NEAR, 128) for g in range(3)]
    s3[...] = jnp.concatenate(turned, axis=1).astype(BF16)
    hop3 = [far_copy(s3.at[lax.rem(far + k, FAR)], r3.at[far], k, sem_3s, sem_3r) for k in range(1, FAR)]
    for copy in hop3:
        copy.start()
    r3[far] = s3[far]
    for copy in hop3:
        copy.wait()
    mid3[...] = r3[...].astype(F32).reshape(FAR * 24, 128)
    for y in range(NEAR):
        s4[y] = jnp.concatenate(
            [mid3[pl.ds(g * 8 + y, FAR, stride=24), :] for g in range(3)], axis=1
        ).astype(BF16)
    hop4 = [near_copy(s4.at[lax.rem(near + k, NEAR)], r4.at[near], k, sem_4s, sem_4r) for k in range(1, NEAR)]
    for copy in hop4:
        copy.start()
    r4[near] = s4[near]
    for copy in hop4:
        copy.wait()

    arrived = r4[...].reshape(128, QUARTER).astype(F32)
    for g in range(3):
        flat[g * 128 : (g + 1) * 128, :] = arrived[:, g * 128 : (g + 1) * 128].T
    lhs = jnp.concatenate([flat[b * 96 : (b + 1) * 96, :] for b in range(4)], axis=1).astype(BF16)
    first_pair = lax.rem(lax.broadcasted_iota(jnp.int32, (96, PADDED), 0), 2) == 0
    nonlinear = jnp.where(first_pair, nt(lhs, masked[0]), nt(lhs, masked[1]))
    for f in range(3):
        own = st[f * 8 : (f + 1) * 8, :] * (2.0 / diffusion[f])
        drives, swapped = [], []
        for i in range(SLABS):
            start = f * 32 + i * 8
            mine = (slab == i).astype(F32)
            drive = nonlinear[start : start + 8] * coupling[f] + own * mine
            drives.append(drive)
            swapped.append(pltpu.roll(drive, 4, 0))
        for i in range(SLABS):
            value = inv[f, 0, i, 0] * drives[0] + inv[f, 1, i, 0] * swapped[0]
            for j in range(1, SLABS):
                value = value + inv[f, 0, i, j] * drives[j] + inv[f, 1, i, j] * swapped[j]
            send_x[i, f * 8 : (f + 1) * 8, :] = value
    last = [x_copy(send_x.at[lax.rem(slab + k, SLABS)], recv_x.at[k - 1], k, sem_us, sem_ur) for k in range(1, SLABS)]
    for copy in last:
        copy.start()
    total[...] = send_x[slab] - st[...]
    for copy in last:
        copy.wait()
    total[...] = total[...] + recv_x[0] + recv_x[1] + recv_x[2]
    for f in range(3):
        for s in range(2):
            for c in range(2):
                for p in range(2):
                    row = f * 8 + s * 4 + c * 2 + p
                    out[p, f, s, c : c + 1, :] = total[row : row + 1, 0:ROWS]


def body(spectral_state, synthesis_table, low_orders, diffusion, coupling):
    low_row = low_orders.reshape(HALF // 2, 2).T.reshape(1, HALF)
    vmem = pl.BlockSpec(memory_space=pltpu.VMEM)
    smem = pl.BlockSpec(memory_space=pltpu.SMEM)
    dma = pltpu.SemaphoreType.DMA
    return pl.pallas_call(
        kernel,
        out_shape=jax.ShapeDtypeStruct(spectral_state.shape, F32),
        in_specs=[vmem, vmem, vmem, smem, smem, smem, pl.BlockSpec(memory_space=pl.ANY)],
        out_specs=vmem,
        scratch_shapes=[
            pltpu.VMEM((8, QUARTER, HALF), BF16),
            pltpu.VMEM((8, QUARTER, HALF), BF16),
            pltpu.VMEM((2, PADDED, 512), BF16),
            pltpu.VMEM((24, PADDED), F32),
            pltpu.VMEM((SLABS, 24, PADDED), BF16),
            pltpu.VMEM((384, 128), F32),
            pltpu.VMEM((NEAR, FAR, 384), BF16),
            pltpu.VMEM((FAR, 24, 128), BF16),
            pltpu.VMEM((NEAR, FAR, 384), BF16),
            pltpu.VMEM((FAR, 24, 128), BF16),
            pltpu.VMEM((FAR, 24, 128), BF16),
            pltpu.VMEM((FAR, 24, 128), BF16),
            pltpu.VMEM((NEAR, FAR, 384), BF16),
            pltpu.VMEM((NEAR, FAR, 384), BF16),
            pltpu.VMEM((3, 128, 128), F32),
            pltpu.VMEM((FAR * 24, 128), F32),
            pltpu.VMEM((3, 2, SLABS, SLABS, 8, PADDED), F32),
            pltpu.VMEM((SLABS, 24, PADDED), F32),
            pltpu.VMEM((SLABS - 1, 24, PADDED), F32),
            pltpu.VMEM((24, PADDED), F32),
            dma,
            dma((SLABS - 1,)), dma((SLABS - 1,)),
            dma((NEAR - 1,)), dma((NEAR - 1,)),
            dma((FAR - 1,)), dma((FAR - 1,)),
            dma((FAR - 1,)), dma((FAR - 1,)),
            dma((NEAR - 1,)), dma((NEAR - 1,)),
            dma((SLABS - 1,)), dma((SLABS - 1,)),
        ],
        compiler_params=pltpu.CompilerParams(
            collective_id=0, has_side_effects=True, vmem_limit_bytes=40 * 1024 * 1024
        ),
    )(spectral_state, synthesis_table, low_row, low_orders, diffusion, coupling, jnp.asarray(wave_tables()))


def solution(mesh):
    placed = (P("mode", None, "radial", None, None), P("mode", None, "radial"), P(), P(), P())
    return jax.shard_map(
        body,
        mesh=mesh,
        in_specs=placed,
        out_specs=P("mode", None, "radial", None, None),
        check_vma=False,
    )
```

```python
import math

import jax
import jax.numpy as jnp
import ml_dtypes
import numpy as np
from jax import lax
from jax.experimental import pallas as pl
from jax.experimental.pallas import tpu as pltpu
from jax.sharding import PartitionSpec as P

inner_radius = 0.538
shell_step = 1.0 / 2048.0

ORDERS = 512
HALF = 256
ROWS = 513
PADDED = 640
NLON = 1536
QUARTER = 384
NLAT = 1024
SLABS = 4
NEAR = 8
FAR = 16
X_STEPS = (2, 1, 3)
NEAR_STEPS = ((2, 0), (2, 1), (1, 0), (3, 0), (1, 1), (3, 1), (0, 1))
FAR_STEPS = (8, 7, 9, 6, 10, 5, 11, 4, 12, 3, 13, 2, 14, 1, 15)
KAPPA = 2.0 * math.sqrt(ORDERS * (ORDERS + 1) / (NLAT * NLON))
MESH = pl.DeviceIdType.MESH
F32 = jnp.float32
BF16 = jnp.bfloat16


def wave_tables():
    low = np.arange(HALF)
    even = np.where(low % 2 == 0, low, ORDERS - 1 - low)
    twice = 2 * np.arange(QUARTER)[:, None] + 1
    heads, tails = [], []
    for order in (even, ORDERS - 1 - even):
        weight = np.where(order == 0, 1.0, 2.0)
        angle = (order[None, :] * twice % (2 * NLON)) * (math.pi / NLON)
        for wave in (weight * np.cos(angle), -weight * np.sin(angle)):
            head = wave.astype(ml_dtypes.bfloat16)
            heads.append(head)
            tails.append((wave - head.astype(np.float64)).astype(ml_dtypes.bfloat16))
    return np.stack(heads + tails)


def nn(a, b):
    return lax.dot_general(a, b, (((1,), (0,)), ((), ())), preferred_element_type=F32)


def nt(a, b):
    return lax.dot_general(a, b, (((1,), (1,)), ((), ())), preferred_element_type=F32)


def kernel(
    state_hbm, table_hbm, low_hbm, lows_hbm, diffusion_hbm, coupling_hbm, waves, out,
    state, table, low_row, lows, diffusion, coupling,
    wave_raw, wave_own, masked, st, cg, flat, s1, s2, r1, r2, s3, r3, s4, r4, mid, mid3, inv, send_x, recv_x, total,
    load_sem, sem_cs, sem_cr, sem_1s, sem_1r, sem_2s, sem_2r, sem_3s, sem_3r, sem_4s, sem_4r, sem_us, sem_ur,
):
    slab = lax.axis_index("radial")
    mode = lax.axis_index("mode")
    far = mode // NEAR
    near = lax.rem(mode, NEAR)

    def x_peer(step):
        return lax.rem(slab + step, SLABS)

    def near_peer(step):
        return lax.rem(near // 2 + step[0], 4) * 2 + lax.rem(lax.rem(near, 2) + step[1], 2)

    def far_peer(step):
        return lax.rem(far + step, FAR)

    barrier = pltpu.get_barrier_semaphore()
    for step in FAR_STEPS:
        pl.semaphore_signal(barrier, inc=1, device_id=(slab, far_peer(step) * NEAR + near), device_id_type=MESH)
    for step in NEAR_STEPS:
        pl.semaphore_signal(barrier, inc=1, device_id=(slab, far * NEAR + near_peer(step)), device_id_type=MESH)
    for step in X_STEPS:
        pl.semaphore_signal(barrier, inc=1, device_id=(x_peer(step), mode), device_id_type=MESH)

    loads = [
        pltpu.make_async_copy(source, target, load_sem.at[i])
        for i, (source, target) in enumerate(
            (
                (lows_hbm, lows), (diffusion_hbm, diffusion), (coupling_hbm, coupling), (state_hbm, state),
                (table_hbm, table), (low_hbm, low_row), (waves, wave_raw),
            )
        )
    ]
    for load in loads:
        load.start()

    st[...] = jnp.zeros_like(st)
    for load in loads[:4]:
        load.wait()
    for f in range(3):
        for s in range(2):
            for c in range(2):
                for p in range(2):
                    row = f * 8 + s * 4 + c * 2 + p
                    st[row : row + 1, 0:ROWS] = state[p, f, s, c : c + 1, :]
    cg[slab] = st[...].astype(BF16)

    def x_copy(source, target, i, send, recv):
        return pltpu.make_async_remote_copy(
            src_ref=source, dst_ref=target, send_sem=send.at[i], recv_sem=recv.at[i],
            device_id=(x_peer(X_STEPS[i]), mode), device_id_type=MESH,
        )

    def near_copies(source, target, send, recv):
        return [
            pltpu.make_async_remote_copy(
                src_ref=source.at[near_peer(step)], dst_ref=target.at[near], send_sem=send.at[i], recv_sem=recv.at[i],
                device_id=(slab, far * NEAR + near_peer(step)), device_id_type=MESH,
            )
            for i, step in enumerate(NEAR_STEPS)
        ]

    def far_copies(source, target, send, recv):
        return [
            pltpu.make_async_remote_copy(
                src_ref=source.at[far_peer(step)], dst_ref=target.at[far], send_sem=send.at[i], recv_sem=recv.at[i],
                device_id=(slab, far_peer(step) * NEAR + near), device_id_type=MESH,
            )
            for i, step in enumerate(FAR_STEPS)
        ]

    loads[4].wait()
    for p in range(2):
        low = lows[mode * 2 + p]
        low_even = lax.rem(low, 2) == 0
        for start, size in ((0, 512), (512, 128)):
            row = lax.broadcasted_iota(jnp.int32, (size, 128), 0) + start
            if start == 0:
                values = table[p, 0:512, :].astype(F32)
            else:
                last = table[p, 512:513, :].astype(F32)
                values = jnp.where(row == 512, jnp.broadcast_to(last, (128, 128)), 0.0)
            in_lower = row < ORDERS - low
            even_order = in_lower == low_even
            odd_sum = jnp.where(in_lower, lax.rem(row, 2), lax.rem(row + low, 2))
            sign = 1.0 - 2.0 * odd_sum.astype(F32)
            for q in range(2):
                north = jnp.where(even_order == (q == 0), values, 0.0)
                masked[p, start : start + size, q * 128 : (q + 1) * 128] = north.astype(BF16)
                masked[p, start : start + size, (2 + q) * 128 : (3 + q) * 128] = (north * sign).astype(BF16)

    for load in loads[5:]:
        load.wait()
    down = lax.broadcasted_iota(jnp.int32, (HALF, HALF), 0)
    across = lax.broadcasted_iota(jnp.int32, (HALF, HALF), 1)
    regroup = (down == lax.rem(across, 128) * 2 + across // 128).astype(F32).astype(BF16)
    natural = jnp.broadcast_to(low_row[...], (HALF, HALF))
    pick = nn((down == natural).astype(F32).astype(BF16), regroup).astype(BF16)
    lowest = pick[0:1, :].astype(F32)
    for q in range(8):
        wave_own[q] = nn(wave_raw[q], pick).astype(BF16)

    row8 = lax.broadcasted_iota(jnp.int32, (8, PADDED), 0)
    lane8 = lax.broadcasted_iota(jnp.int32, (8, PADDED), 1)
    low8 = jnp.where(lax.rem(row8, 2) == 0, lows[mode * 2], lows[mode * 2 + 1])
    degree = jnp.where(lane8 < ORDERS - low8, low8 + lane8, lane8 - 1).astype(F32)
    degree = degree * (degree + 1.0) * (shell_step * shell_step)
    first_shell = row8 < 4
    for f in range(3):
        diagonal = []
        for s in range(8):
            radius = inner_radius + (s + 0.5) * shell_step
            diagonal.append(degree * (1.0 / (radius * radius)) + (1.0 / diffusion[f] + 2.0))
        leading = [jnp.ones((8, PADDED), F32), diagonal[0]]
        trailing = [jnp.ones((8, PADDED), F32), diagonal[7]]
        for s in range(1, 8):
            leading.append(diagonal[s] * leading[s] - leading[s - 1])
            trailing.append(diagonal[7 - s] * trailing[s] - trailing[s - 1])
        share = 1.0 / leading[8]
        scaled = [value * share for value in leading]

        def entry(i, j):
            return scaled[min(i, j)] * trailing[7 - max(i, j)]

        for i in range(SLABS):
            for j in range(i, SLABS):
                inv[f, 0, i, j] = jnp.where(first_shell, entry(2 * i, 2 * j), entry(2 * i + 1, 2 * j + 1))
                inv[f, 1, i, j] = jnp.where(first_shell, entry(2 * i, 2 * j + 1), entry(2 * i + 1, 2 * j))
                if i != j:
                    inv[f, 0, j, i] = jnp.where(first_shell, entry(2 * i, 2 * j), entry(2 * i + 1, 2 * j + 1))
                    inv[f, 1, j, i] = jnp.where(first_shell, entry(2 * i + 1, 2 * j), entry(2 * i, 2 * j + 1))

    pl.semaphore_wait(barrier, SLABS + NEAR + FAR - 3)

    coefs = [x_copy(cg.at[slab], cg.at[slab], i, sem_cs, sem_cr) for i in range(SLABS - 1)]
    for copy in coefs:
        copy.start()

    for copy in coefs:
        copy.wait()

    gathered = [cg[i].astype(F32) for i in range(SLABS)]
    lhs = jnp.concatenate(
        [gathered[i][f * 8 : (f + 1) * 8] for f in range(3) for i in range(SLABS)], axis=0
    ).astype(BF16)
    first_pair = lax.rem(lax.broadcasted_iota(jnp.int32, (96, 512), 0), 2) == 0
    synth = jnp.where(first_pair, nn(lhs, masked[0]), nn(lhs, masked[1]))
    for b in range(4):
        flat[b * 96 : (b + 1) * 96, :] = synth[:, b * 128 : (b + 1) * 128]
    for g in range(3):
        block = flat[g * 128 : (g + 1) * 128, :].T
        s1[:, :, g * 128 : (g + 1) * 128] = block.reshape(NEAR, FAR, 128).astype(BF16)
    hop1 = near_copies(s1, r1, sem_1s, sem_1r)
    for copy in hop1:
        copy.start()
    r1[near] = s1[near]

    for copy in hop1:
        copy.wait()
    arrived = r1[...].reshape(128, QUARTER).astype(F32)
    for g in range(3):
        mid[g] = arrived[:, g * 128 : (g + 1) * 128]
    for z in range(FAR):
        s2[z] = jnp.concatenate([mid[g, pl.ds(z, NEAR, stride=FAR), :] for g in range(3)], axis=0).astype(BF16)
    hop2 = far_copies(s2, r2, sem_2s, sem_2r)
    for copy in hop2:
        copy.start()
    r2[far] = s2[far]

    for copy in hop2:
        copy.wait()
    arrived = r2[...].astype(F32)
    for g in range(3):
        flat[g * 128 : (g + 1) * 128, :] = arrived[:, g * 8 : (g + 1) * 8, :].reshape(128, 128).T

    parts = []
    for q in range(2):
        for c in range(2):
            rows = [
                jnp.concatenate(
                    [flat[pl.ds((h * 2 + q) * 96 + c * 2 + p, 24, stride=4), :] for p in range(2)], axis=1
                )
                for h in range(2)
            ]
            data = jnp.concatenate(rows, axis=0).astype(BF16)
            at = q * 2 + c
            parts.append(nt(data, wave_own[at]) + nt(data, wave_own[4 + at]))
    a, b = parts[0] + parts[2], parts[1] + parts[3]
    c, d = parts[0] - parts[2], parts[1] - parts[3]
    images = (a + b, a - b, c - d, c + d)
    sums = [[], [], [], []]
    for h in range(2):
        for left, right in ((0, 1), (0, 2), (1, 2)):
            u, v = h * 24 + left * 8, h * 24 + right * 8
            p1, p2, p3, p4 = [image[u : u + 8] * image[v : v + 8] for image in images]
            both, across = p1 + p2, p3 + p4
            turn, twist = p1 - p2, p4 - p3
            sums[0].append(both + across)
            sums[1].append(turn + twist)
            sums[2].append(both - across)
            sums[3].append(turn - twist)
    for q in range(2):
        for c in range(2):
            at = q * 2 + c
            value = jnp.concatenate(sums[at], axis=0)
            head = value.astype(BF16)
            tail = (value - head.astype(F32)).astype(BF16)
            answer = nn(head, wave_own[at]) + (nn(tail, wave_own[at]) + nn(head, wave_own[4 + at]))
            if q == 0:
                answer = answer * (0.5 * KAPPA * (1.0 + lowest))
            else:
                answer = answer * (0.5 * KAPPA)
            for h in range(2):
                for p in range(2):
                    flat[pl.ds((h * 2 + q) * 96 + c * 2 + p, 24, stride=4), :] = answer[
                        h * 24 : (h + 1) * 24, p * 128 : (p + 1) * 128
                    ]
    turned = [flat[g * 128 : (g + 1) * 128, :].T.reshape(FAR, NEAR, 128) for g in range(3)]
    s3[...] = jnp.concatenate(turned, axis=1).astype(BF16)
    hop3 = far_copies(s3, r3, sem_3s, sem_3r)
    for copy in hop3:
        copy.start()
    r3[far] = s3[far]
    for copy in hop3:
        copy.wait()
    mid3[...] = r3[...].astype(F32).reshape(FAR * 24, 128)
    for y in range(NEAR):
        s4[y] = jnp.concatenate(
            [mid3[pl.ds(g * 8 + y, FAR, stride=24), :] for g in range(3)], axis=1
        ).astype(BF16)
    hop4 = near_copies(s4, r4, sem_4s, sem_4r)
    for copy in hop4:
        copy.start()
    r4[near] = s4[near]
    for copy in hop4:
        copy.wait()

    arrived = r4[...].reshape(128, QUARTER).astype(F32)
    for g in range(3):
        flat[g * 128 : (g + 1) * 128, :] = arrived[:, g * 128 : (g + 1) * 128].T
    lhs = jnp.concatenate([flat[b * 96 : (b + 1) * 96, :] for b in range(4)], axis=1).astype(BF16)
    first_pair = lax.rem(lax.broadcasted_iota(jnp.int32, (96, PADDED), 0), 2) == 0
    nonlinear = jnp.where(first_pair, nt(lhs, masked[0]), nt(lhs, masked[1]))
    for f in range(3):
        own = st[f * 8 : (f + 1) * 8, :] * (2.0 / diffusion[f])
        drives, swapped = [], []
        for i in range(SLABS):
            start = f * 32 + i * 8
            mine = (slab == i).astype(F32)
            drive = nonlinear[start : start + 8] * coupling[f] + own * mine
            drives.append(drive)
            swapped.append(pltpu.roll(drive, 4, 0))
        for i in range(SLABS):
            value = inv[f, 0, i, 0] * drives[0] + inv[f, 1, i, 0] * swapped[0]
            for j in range(1, SLABS):
                value = value + inv[f, 0, i, j] * drives[j] + inv[f, 1, i, j] * swapped[j]
            send_x[i, f * 8 : (f + 1) * 8, :] = value
    last = [x_copy(send_x.at[x_peer(X_STEPS[i])], recv_x.at[i], i, sem_us, sem_ur) for i in range(SLABS - 1)]
    for copy in last:
        copy.start()
    total[...] = send_x[slab] - st[...]
    for copy in last:
        copy.wait()
    total[...] = total[...] + recv_x[0] + recv_x[1] + recv_x[2]
    for f in range(3):
        for s in range(2):
            for c in range(2):
                for p in range(2):
                    row = f * 8 + s * 4 + c * 2 + p
                    out[p, f, s, c : c + 1, :] = total[row : row + 1, 0:ROWS]


def body(spectral_state, synthesis_table, low_orders, diffusion, coupling):
    low_row = low_orders.reshape(1, HALF)
    vmem = pl.BlockSpec(memory_space=pltpu.VMEM)
    hbm = pl.BlockSpec(memory_space=pltpu.HBM)
    dma = pltpu.SemaphoreType.DMA
    return pl.pallas_call(
        kernel,
        out_shape=jax.ShapeDtypeStruct(spectral_state.shape, F32),
        in_specs=[hbm] * 7,
        out_specs=vmem,
        scratch_shapes=[
            pltpu.VMEM(spectral_state.shape, F32),
            pltpu.VMEM(synthesis_table.shape, BF16),
            pltpu.VMEM((1, HALF), jnp.int32),
            pltpu.SMEM((HALF,), jnp.int32),
            pltpu.SMEM((3,), F32),
            pltpu.SMEM((3,), F32),
            pltpu.VMEM((8, QUARTER, HALF), BF16),
            pltpu.VMEM((8, QUARTER, HALF), BF16),
            pltpu.VMEM((2, PADDED, 512), BF16),
            pltpu.VMEM((24, PADDED), F32),
            pltpu.VMEM((SLABS, 24, PADDED), BF16),
            pltpu.VMEM((384, 128), F32),
            pltpu.VMEM((NEAR, FAR, 384), BF16),
            pltpu.VMEM((FAR, 24, 128), BF16),
            pltpu.VMEM((NEAR, FAR, 384), BF16),
            pltpu.VMEM((FAR, 24, 128), BF16),
            pltpu.VMEM((FAR, 24, 128), BF16),
            pltpu.VMEM((FAR, 24, 128), BF16),
            pltpu.VMEM((NEAR, FAR, 384), BF16),
            pltpu.VMEM((NEAR, FAR, 384), BF16),
            pltpu.VMEM((3, 128, 128), F32),
            pltpu.VMEM((FAR * 24, 128), F32),
            pltpu.VMEM((3, 2, SLABS, SLABS, 8, PADDED), F32),
            pltpu.VMEM((SLABS, 24, PADDED), F32),
            pltpu.VMEM((SLABS - 1, 24, PADDED), F32),
            pltpu.VMEM((24, PADDED), F32),
            dma((7,)),
            dma((SLABS - 1,)), dma((SLABS - 1,)),
            dma((NEAR - 1,)), dma((NEAR - 1,)),
            dma((FAR - 1,)), dma((FAR - 1,)),
            dma((FAR - 1,)), dma((FAR - 1,)),
            dma((NEAR - 1,)), dma((NEAR - 1,)),
            dma((SLABS - 1,)), dma((SLABS - 1,)),
        ],
        compiler_params=pltpu.CompilerParams(
            collective_id=0, has_side_effects=True, vmem_limit_bytes=63 * 1024 * 1024
        ),
    )(spectral_state, synthesis_table, low_row, low_orders, diffusion, coupling, jnp.asarray(wave_tables()))


def solution(mesh):
    placed = (P("mode", None, "radial", None, None), P("mode", None, "radial"), P(), P(), P())
    return jax.shard_map(
        body,
        mesh=mesh,
        in_specs=placed,
        out_specs=P("mode", None, "radial", None, None),
        check_vma=False,
    )
```

```python
import math

import jax
import jax.numpy as jnp
import ml_dtypes
import numpy as np
from jax import lax
from jax.experimental import pallas as pl
from jax.experimental.pallas import tpu as pltpu
from jax.sharding import PartitionSpec as P

inner_radius = 0.538
shell_step = 1.0 / 2048.0

ORDERS = 512
HALF = 256
ROWS = 513
PADDED = 640
NLON = 1536
QUARTER = 384
NLAT = 1024
SLABS = 4
NEAR = 8
FAR = 16
X_STEPS = (2, 1, 3)
NEAR_STEPS = ((2, 0), (2, 1), (1, 0), (3, 0), (1, 1), (3, 1), (0, 1))
FAR_STEPS = (8, 7, 9, 6, 10, 5, 11, 4, 12, 3, 13, 2, 14, 1, 15)
GREETED = (2, 14, 1, 15)
KAPPA = 2.0 * math.sqrt(ORDERS * (ORDERS + 1) / (NLAT * NLON))
MESH = pl.DeviceIdType.MESH
F32 = jnp.float32
BF16 = jnp.bfloat16


def wave_tables():
    low = np.arange(HALF)
    even = np.where(low % 2 == 0, low, ORDERS - 1 - low)
    twice = 2 * np.arange(QUARTER)[:, None] + 1
    heads, tails = [], []
    for order in (even, ORDERS - 1 - even):
        weight = np.where(order == 0, 1.0, 2.0)
        angle = (order[None, :] * twice % (2 * NLON)) * (math.pi / NLON)
        for wave in (weight * np.cos(angle), -weight * np.sin(angle)):
            head = wave.astype(ml_dtypes.bfloat16)
            heads.append(head)
            tails.append((wave - head.astype(np.float64)).astype(ml_dtypes.bfloat16))
    return np.stack(heads + tails)


def nn(a, b):
    return lax.dot_general(a, b, (((1,), (0,)), ((), ())), preferred_element_type=F32)


def nt(a, b):
    return lax.dot_general(a, b, (((1,), (1,)), ((), ())), preferred_element_type=F32)


def kernel(
    state_hbm, table_hbm, low_hbm, lows_hbm, diffusion_hbm, coupling_hbm, waves, out,
    state, table, low_row, lows, diffusion, coupling,
    wave_raw, wave_own, masked, st, cg, flat, s1, s2, r1, r2, s3, r3, s4, r4, mid, mid3, inv, send_x, recv_x, total,
    relay, load_sem, sem_cs, sem_cr, sem_1s, sem_1r, sem_2s, sem_2r, sem_3s, sem_3r, sem_4s, sem_4r, sem_us, sem_ur,
):
    slab = lax.axis_index("radial")
    mode = lax.axis_index("mode")
    far = mode // NEAR
    near = lax.rem(mode, NEAR)

    def x_peer(step):
        return lax.rem(slab + step, SLABS)

    def near_peer(step):
        return lax.rem(near // 2 + step[0], 4) * 2 + lax.rem(lax.rem(near, 2) + step[1], 2)

    def far_peer(step):
        return lax.rem(far + step, FAR)

    barrier = pltpu.get_barrier_semaphore()
    for step in GREETED:
        pl.semaphore_signal(barrier, inc=1, device_id=(slab, far_peer(step) * NEAR + near), device_id_type=MESH)
    for step in NEAR_STEPS:
        pl.semaphore_signal(barrier, inc=1, device_id=(slab, far * NEAR + near_peer(step)), device_id_type=MESH)
    for step in X_STEPS:
        pl.semaphore_signal(barrier, inc=1, device_id=(x_peer(step), mode), device_id_type=MESH)

    loads = [
        pltpu.make_async_copy(source, target, load_sem.at[i])
        for i, (source, target) in enumerate(
            (
                (lows_hbm, lows), (diffusion_hbm, diffusion), (coupling_hbm, coupling), (state_hbm, state),
                (table_hbm, table), (low_hbm, low_row), (waves, wave_raw),
            )
        )
    ]
    for load in loads:
        load.start()

    st[...] = jnp.zeros_like(st)
    for load in loads[:4]:
        load.wait()
    for f in range(3):
        for s in range(2):
            for c in range(2):
                for p in range(2):
                    row = f * 8 + s * 4 + c * 2 + p
                    st[row : row + 1, 0:ROWS] = state[p, f, s, c : c + 1, :]
    cg[slab] = st[...].astype(BF16)

    def x_copy(source, target, i, send, recv):
        return pltpu.make_async_remote_copy(
            src_ref=source, dst_ref=target, send_sem=send.at[i], recv_sem=recv.at[i],
            device_id=(x_peer(X_STEPS[i]), mode), device_id_type=MESH,
        )

    def near_copies(source, target, send, recv):
        return [
            pltpu.make_async_remote_copy(
                src_ref=source.at[near_peer(step)], dst_ref=target.at[near], send_sem=send.at[i], recv_sem=recv.at[i],
                device_id=(slab, far * NEAR + near_peer(step)), device_id_type=MESH,
            )
            for i, step in enumerate(NEAR_STEPS)
        ]

    def far_copies(source, target, send, recv):
        return [
            pltpu.make_async_remote_copy(
                src_ref=source.at[far_peer(step)], dst_ref=target.at[far], send_sem=send.at[i], recv_sem=recv.at[i],
                device_id=(slab, far_peer(step) * NEAR + near), device_id_type=MESH,
            )
            for i, step in enumerate(FAR_STEPS)
        ]

    loads[4].wait()
    for p in range(2):
        low = lows[mode * 2 + p]
        low_even = lax.rem(low, 2) == 0
        for start, size in ((0, 512), (512, 128)):
            row = lax.broadcasted_iota(jnp.int32, (size, 128), 0) + start
            if start == 0:
                values = table[p, 0:512, :].astype(F32)
            else:
                last = table[p, 512:513, :].astype(F32)
                values = jnp.where(row == 512, jnp.broadcast_to(last, (128, 128)), 0.0)
            in_lower = row < ORDERS - low
            even_order = in_lower == low_even
            odd_sum = jnp.where(in_lower, lax.rem(row, 2), lax.rem(row + low, 2))
            sign = 1.0 - 2.0 * odd_sum.astype(F32)
            for q in range(2):
                north = jnp.where(even_order == (q == 0), values, 0.0)
                masked[p, start : start + size, q * 128 : (q + 1) * 128] = north.astype(BF16)
                masked[p, start : start + size, (2 + q) * 128 : (3 + q) * 128] = (north * sign).astype(BF16)

    pl.semaphore_wait(barrier, SLABS - 1 + NEAR - 1 + len(GREETED))

    coefs = [x_copy(cg.at[slab], cg.at[slab], i, sem_cs, sem_cr) for i in range(SLABS - 1)]
    for copy in coefs:
        copy.start()

    def pass_on(i, reach):
        for step in (reach, FAR - reach):
            pl.semaphore_signal(relay.at[i], inc=1, device_id=(slab, far_peer(step) * NEAR + near), device_id_type=MESH)

    pass_on(0, 2)

    for load in loads[5:]:
        load.wait()
    down = lax.broadcasted_iota(jnp.int32, (HALF, HALF), 0)
    across = lax.broadcasted_iota(jnp.int32, (HALF, HALF), 1)
    regroup = (down == lax.rem(across, 128) * 2 + across // 128).astype(F32).astype(BF16)
    natural = jnp.broadcast_to(low_row[...], (HALF, HALF))
    pick = nn((down == natural).astype(F32).astype(BF16), regroup).astype(BF16)
    lowest = pick[0:1, :].astype(F32)
    for q in range(8):
        wave_own[q] = nn(wave_raw[q], pick).astype(BF16)

    pl.semaphore_wait(relay.at[0], 2)
    pass_on(1, 4)

    for copy in coefs:
        copy.wait()

    gathered = [cg[i].astype(F32) for i in range(SLABS)]
    lhs = jnp.concatenate(
        [gathered[i][f * 8 : (f + 1) * 8] for f in range(3) for i in range(SLABS)], axis=0
    ).astype(BF16)
    first_pair = lax.rem(lax.broadcasted_iota(jnp.int32, (96, 512), 0), 2) == 0
    synth = jnp.where(first_pair, nn(lhs, masked[0]), nn(lhs, masked[1]))
    for b in range(4):
        flat[b * 96 : (b + 1) * 96, :] = synth[:, b * 128 : (b + 1) * 128]
    for g in range(3):
        block = flat[g * 128 : (g + 1) * 128, :].T
        s1[:, :, g * 128 : (g + 1) * 128] = block.reshape(NEAR, FAR, 128).astype(BF16)
    hop1 = near_copies(s1, r1, sem_1s, sem_1r)
    for copy in hop1:
        copy.start()
    r1[near] = s1[near]

    row8 = lax.broadcasted_iota(jnp.int32, (8, PADDED), 0)
    lane8 = lax.broadcasted_iota(jnp.int32, (8, PADDED), 1)
    low8 = jnp.where(lax.rem(row8, 2) == 0, lows[mode * 2], lows[mode * 2 + 1])
    degree = jnp.where(lane8 < ORDERS - low8, low8 + lane8, lane8 - 1).astype(F32)
    degree = degree * (degree + 1.0) * (shell_step * shell_step)
    first_shell = row8 < 4
    for f in range(3):
        diagonal = []
        for s in range(8):
            radius = inner_radius + (s + 0.5) * shell_step
            diagonal.append(degree * (1.0 / (radius * radius)) + (1.0 / diffusion[f] + 2.0))
        leading = [jnp.ones((8, PADDED), F32), diagonal[0]]
        trailing = [jnp.ones((8, PADDED), F32), diagonal[7]]
        for s in range(1, 8):
            leading.append(diagonal[s] * leading[s] - leading[s - 1])
            trailing.append(diagonal[7 - s] * trailing[s] - trailing[s - 1])
        share = 1.0 / leading[8]
        scaled = [value * share for value in leading]

        def entry(i, j):
            return scaled[min(i, j)] * trailing[7 - max(i, j)]

        for i in range(SLABS):
            for j in range(i, SLABS):
                inv[f, 0, i, j] = jnp.where(first_shell, entry(2 * i, 2 * j), entry(2 * i + 1, 2 * j + 1))
                inv[f, 1, i, j] = jnp.where(first_shell, entry(2 * i, 2 * j + 1), entry(2 * i + 1, 2 * j))
                if i != j:
                    inv[f, 0, j, i] = jnp.where(first_shell, entry(2 * i, 2 * j), entry(2 * i + 1, 2 * j + 1))
                    inv[f, 1, j, i] = jnp.where(first_shell, entry(2 * i + 1, 2 * j), entry(2 * i, 2 * j + 1))


    for copy in hop1:
        copy.wait()
    arrived = r1[...].reshape(128, QUARTER).astype(F32)
    for g in range(3):
        mid[g] = arrived[:, g * 128 : (g + 1) * 128]
    for z in range(FAR):
        s2[z] = jnp.concatenate([mid[g, pl.ds(z, NEAR, stride=FAR), :] for g in range(3)], axis=0).astype(BF16)
    pl.semaphore_wait(relay.at[1], 2)
    hop2 = far_copies(s2, r2, sem_2s, sem_2r)
    for copy in hop2:
        copy.start()
    r2[far] = s2[far]

    for copy in hop2:
        copy.wait()
    arrived = r2[...].astype(F32)
    for g in range(3):
        flat[g * 128 : (g + 1) * 128, :] = arrived[:, g * 8 : (g + 1) * 8, :].reshape(128, 128).T

    parts = []
    for q in range(2):
        for c in range(2):
            rows = [
                jnp.concatenate(
                    [flat[pl.ds((h * 2 + q) * 96 + c * 2 + p, 24, stride=4), :] for p in range(2)], axis=1
                )
                for h in range(2)
            ]
            data = jnp.concatenate(rows, axis=0).astype(BF16)
            at = q * 2 + c
            parts.append(nt(data, wave_own[at]) + nt(data, wave_own[4 + at]))
    a, b = parts[0] + parts[2], parts[1] + parts[3]
    c, d = parts[0] - parts[2], parts[1] - parts[3]
    images = (a + b, a - b, c - d, c + d)
    sums = [[], [], [], []]
    for h in range(2):
        for left, right in ((0, 1), (0, 2), (1, 2)):
            u, v = h * 24 + left * 8, h * 24 + right * 8
            p1, p2, p3, p4 = [image[u : u + 8] * image[v : v + 8] for image in images]
            both, across = p1 + p2, p3 + p4
            turn, twist = p1 - p2, p4 - p3
            sums[0].append(both + across)
            sums[1].append(turn + twist)
            sums[2].append(both - across)
            sums[3].append(turn - twist)
    for q in range(2):
        for c in range(2):
            at = q * 2 + c
            value = jnp.concatenate(sums[at], axis=0)
            head = value.astype(BF16)
            tail = (value - head.astype(F32)).astype(BF16)
            answer = nn(head, wave_own[at]) + (nn(tail, wave_own[at]) + nn(head, wave_own[4 + at]))
            if q == 0:
                answer = answer * (0.5 * KAPPA * (1.0 + lowest))
            else:
                answer = answer * (0.5 * KAPPA)
            for h in range(2):
                for p in range(2):
                    flat[pl.ds((h * 2 + q) * 96 + c * 2 + p, 24, stride=4), :] = answer[
                        h * 24 : (h + 1) * 24, p * 128 : (p + 1) * 128
                    ]
    turned = [flat[g * 128 : (g + 1) * 128, :].T.reshape(FAR, NEAR, 128) for g in range(3)]
    s3[...] = jnp.concatenate(turned, axis=1).astype(BF16)
    hop3 = far_copies(s3, r3, sem_3s, sem_3r)
    for copy in hop3:
        copy.start()
    r3[far] = s3[far]
    for copy in hop3:
        copy.wait()
    mid3[...] = r3[...].astype(F32).reshape(FAR * 24, 128)
    for y in range(NEAR):
        s4[y] = jnp.concatenate(
            [mid3[pl.ds(g * 8 + y, FAR, stride=24), :] for g in range(3)], axis=1
        ).astype(BF16)
    hop4 = near_copies(s4, r4, sem_4s, sem_4r)
    for copy in hop4:
        copy.start()
    r4[near] = s4[near]
    for copy in hop4:
        copy.wait()

    arrived = r4[...].reshape(128, QUARTER).astype(F32)
    for g in range(3):
        flat[g * 128 : (g + 1) * 128, :] = arrived[:, g * 128 : (g + 1) * 128].T
    lhs = jnp.concatenate([flat[b * 96 : (b + 1) * 96, :] for b in range(4)], axis=1).astype(BF16)
    first_pair = lax.rem(lax.broadcasted_iota(jnp.int32, (96, PADDED), 0), 2) == 0
    nonlinear = jnp.where(first_pair, nt(lhs, masked[0]), nt(lhs, masked[1]))
    for f in range(3):
        own = st[f * 8 : (f + 1) * 8, :] * (2.0 / diffusion[f])
        drives, swapped = [], []
        for i in range(SLABS):
            start = f * 32 + i * 8
            mine = (slab == i).astype(F32)
            drive = nonlinear[start : start + 8] * coupling[f] + own * mine
            drives.append(drive)
            swapped.append(pltpu.roll(drive, 4, 0))
        for i in range(SLABS):
            value = inv[f, 0, i, 0] * drives[0] + inv[f, 1, i, 0] * swapped[0]
            for j in range(1, SLABS):
                value = value + inv[f, 0, i, j] * drives[j] + inv[f, 1, i, j] * swapped[j]
            send_x[i, f * 8 : (f + 1) * 8, :] = value
    last = [x_copy(send_x.at[x_peer(X_STEPS[i])], recv_x.at[i], i, sem_us, sem_ur) for i in range(SLABS - 1)]
    for copy in last:
        copy.start()
    total[...] = send_x[slab] - st[...]
    for copy in last:
        copy.wait()
    total[...] = total[...] + recv_x[0] + recv_x[1] + recv_x[2]
    for f in range(3):
        for s in range(2):
            for c in range(2):
                for p in range(2):
                    row = f * 8 + s * 4 + c * 2 + p
                    out[p, f, s, c : c + 1, :] = total[row : row + 1, 0:ROWS]


def body(spectral_state, synthesis_table, low_orders, diffusion, coupling):
    low_row = low_orders.reshape(1, HALF)
    vmem = pl.BlockSpec(memory_space=pltpu.VMEM)
    hbm = pl.BlockSpec(memory_space=pltpu.HBM)
    dma = pltpu.SemaphoreType.DMA
    return pl.pallas_call(
        kernel,
        out_shape=jax.ShapeDtypeStruct(spectral_state.shape, F32),
        in_specs=[hbm] * 7,
        out_specs=vmem,
        scratch_shapes=[
            pltpu.VMEM(spectral_state.shape, F32),
            pltpu.VMEM(synthesis_table.shape, BF16),
            pltpu.VMEM((1, HALF), jnp.int32),
            pltpu.SMEM((HALF,), jnp.int32),
            pltpu.SMEM((3,), F32),
            pltpu.SMEM((3,), F32),
            pltpu.VMEM((8, QUARTER, HALF), BF16),
            pltpu.VMEM((8, QUARTER, HALF), BF16),
            pltpu.VMEM((2, PADDED, 512), BF16),
            pltpu.VMEM((24, PADDED), F32),
            pltpu.VMEM((SLABS, 24, PADDED), BF16),
            pltpu.VMEM((384, 128), F32),
            pltpu.VMEM((NEAR, FAR, 384), BF16),
            pltpu.VMEM((FAR, 24, 128), BF16),
            pltpu.VMEM((NEAR, FAR, 384), BF16),
            pltpu.VMEM((FAR, 24, 128), BF16),
            pltpu.VMEM((FAR, 24, 128), BF16),
            pltpu.VMEM((FAR, 24, 128), BF16),
            pltpu.VMEM((NEAR, FAR, 384), BF16),
            pltpu.VMEM((NEAR, FAR, 384), BF16),
            pltpu.VMEM((3, 128, 128), F32),
            pltpu.VMEM((FAR * 24, 128), F32),
            pltpu.VMEM((3, 2, SLABS, SLABS, 8, PADDED), F32),
            pltpu.VMEM((SLABS, 24, PADDED), F32),
            pltpu.VMEM((SLABS - 1, 24, PADDED), F32),
            pltpu.VMEM((24, PADDED), F32),
            pltpu.SemaphoreType.REGULAR((2,)),
            dma((7,)),
            dma((SLABS - 1,)), dma((SLABS - 1,)),
            dma((NEAR - 1,)), dma((NEAR - 1,)),
            dma((FAR - 1,)), dma((FAR - 1,)),
            dma((FAR - 1,)), dma((FAR - 1,)),
            dma((NEAR - 1,)), dma((NEAR - 1,)),
            dma((SLABS - 1,)), dma((SLABS - 1,)),
        ],
        compiler_params=pltpu.CompilerParams(
            collective_id=0, has_side_effects=True, vmem_limit_bytes=63 * 1024 * 1024
        ),
    )(spectral_state, synthesis_table, low_row, low_orders, diffusion, coupling, jnp.asarray(wave_tables()))


def solution(mesh):
    placed = (P("mode", None, "radial", None, None), P("mode", None, "radial"), P(), P(), P())
    return jax.shard_map(
        body,
        mesh=mesh,
        in_specs=placed,
        out_specs=P("mode", None, "radial", None, None),
        check_vma=False,
    )
```

```python
import math

import jax
import jax.numpy as jnp
import ml_dtypes
import numpy as np
from jax import lax
from jax.experimental import pallas as pl
from jax.experimental.pallas import tpu as pltpu
from jax.sharding import PartitionSpec as P

inner_radius = 0.538
shell_step = 1.0 / 2048.0

ORDERS = 512
HALF = 256
ROWS = 513
PADDED = 640
NLON = 1536
QUARTER = 384
NLAT = 1024
SLABS = 4
NEAR = 8
FAR = 16
X_STEPS = (2, 1, 3)
NEAR_STEPS = ((2, 0), (2, 1), (1, 0), (3, 0), (1, 1), (3, 1), (0, 1))
FAR_STEPS = (8, 7, 9, 6, 10, 5, 11, 4, 12, 3, 13, 2, 14, 1, 15)
GREETED = (2, 14, 1, 15)
KAPPA = 2.0 * math.sqrt(ORDERS * (ORDERS + 1) / (NLAT * NLON))
MESH = pl.DeviceIdType.MESH
F32 = jnp.float32
BF16 = jnp.bfloat16


def wave_tables():
    low = np.arange(HALF)
    even = np.where(low % 2 == 0, low, ORDERS - 1 - low)
    twice = 2 * np.arange(QUARTER)[:, None] + 1
    heads, tails = [], []
    for order in (even, ORDERS - 1 - even):
        weight = np.where(order == 0, 1.0, 2.0)
        angle = (order[None, :] * twice % (2 * NLON)) * (math.pi / NLON)
        for wave in (weight * np.cos(angle), -weight * np.sin(angle)):
            head = wave.astype(ml_dtypes.bfloat16)
            heads.append(head)
            tails.append((wave - head.astype(np.float64)).astype(ml_dtypes.bfloat16))
    return np.stack(heads + tails)


def nn(a, b):
    return lax.dot_general(a, b, (((1,), (0,)), ((), ())), preferred_element_type=F32)


def nt(a, b):
    return lax.dot_general(a, b, (((1,), (1,)), ((), ())), preferred_element_type=F32)


def kernel(
    state_hbm, table_hbm, low_hbm, lows_hbm, diffusion_hbm, coupling_hbm, waves, out,
    state, table, rows, low_row, lows, diffusion, coupling,
    wave_raw, wave_own, masked, st, cg, flat, s1, s2, r1, r2, s3, r3, s4, r4, mid, mid3, inv, send_x, recv_x, total,
    relay, load_sem, sem_cs, sem_cr, sem_1s, sem_1r, sem_2s, sem_2r, sem_3s, sem_3r, sem_4s, sem_4r, sem_us, sem_ur,
):
    slab = lax.axis_index("radial")
    mode = lax.axis_index("mode")
    far = mode // NEAR
    near = lax.rem(mode, NEAR)

    def x_peer(step):
        return lax.rem(slab + step, SLABS)

    def near_peer(step):
        return lax.rem(near // 2 + step[0], 4) * 2 + lax.rem(lax.rem(near, 2) + step[1], 2)

    def far_peer(step):
        return lax.rem(far + step, FAR)

    barrier = pltpu.get_barrier_semaphore()
    for step in GREETED:
        pl.semaphore_signal(barrier, inc=1, device_id=(slab, far_peer(step) * NEAR + near), device_id_type=MESH)
    for step in NEAR_STEPS:
        pl.semaphore_signal(barrier, inc=1, device_id=(slab, far * NEAR + near_peer(step)), device_id_type=MESH)
    for step in X_STEPS:
        pl.semaphore_signal(barrier, inc=1, device_id=(x_peer(step), mode), device_id_type=MESH)

    loads = [
        pltpu.make_async_copy(source, target, load_sem.at[i])
        for i, (source, target) in enumerate(
            (
                (lows_hbm, lows), (diffusion_hbm, diffusion), (coupling_hbm, coupling), (state_hbm, state),
                (table_hbm, table), (low_hbm, low_row), (waves, wave_raw),
            )
        )
    ]
    for load in loads:
        load.start()

    st[...] = jnp.zeros_like(st)
    for load in loads[:4]:
        load.wait()
    for f in range(3):
        for s in range(2):
            for c in range(2):
                for p in range(2):
                    row = f * 8 + s * 4 + c * 2 + p
                    st[row : row + 1, 0:ROWS] = state[p, f, s, c : c + 1, :]
    cg[slab] = st[...].astype(BF16)

    def x_copy(source, target, i, send, recv):
        return pltpu.make_async_remote_copy(
            src_ref=source, dst_ref=target, send_sem=send.at[i], recv_sem=recv.at[i],
            device_id=(x_peer(X_STEPS[i]), mode), device_id_type=MESH,
        )

    def near_copies(source, target, send, recv):
        return [
            pltpu.make_async_remote_copy(
                src_ref=source.at[near_peer(step)], dst_ref=target.at[near], send_sem=send.at[i], recv_sem=recv.at[i],
                device_id=(slab, far * NEAR + near_peer(step)), device_id_type=MESH,
            )
            for i, step in enumerate(NEAR_STEPS)
        ]

    def far_copies(source, target, send, recv):
        return [
            pltpu.make_async_remote_copy(
                src_ref=source.at[far_peer(step)], dst_ref=target.at[far], send_sem=send.at[i], recv_sem=recv.at[i],
                device_id=(slab, far_peer(step) * NEAR + near), device_id_type=MESH,
            )
            for i, step in enumerate(FAR_STEPS)
        ]

    loads[4].wait()
    rows[...] = table[...].astype(F32).reshape(2 * ROWS, 128)
    for p in range(2):
        low = lows[mode * 2 + p]
        low_even = lax.rem(low, 2) == 0
        for start, size in ((0, 512), (512, 128)):
            row = lax.broadcasted_iota(jnp.int32, (size, 128), 0) + start
            if start == 0:
                values = rows[pl.ds(p, 512, stride=2), :]
            else:
                last = rows[1024 + p : 1025 + p, :]
                values = jnp.where(row == 512, jnp.broadcast_to(last, (128, 128)), 0.0)
            in_lower = row < ORDERS - low
            even_order = in_lower == low_even
            odd_sum = jnp.where(in_lower, lax.rem(row, 2), lax.rem(row + low, 2))
            sign = 1.0 - 2.0 * odd_sum.astype(F32)
            for q in range(2):
                north = jnp.where(even_order == (q == 0), values, 0.0)
                masked[p, start : start + size, q * 128 : (q + 1) * 128] = north.astype(BF16)
                masked[p, start : start + size, (2 + q) * 128 : (3 + q) * 128] = (north * sign).astype(BF16)

    pl.semaphore_wait(barrier, SLABS - 1 + NEAR - 1 + len(GREETED))

    coefs = [x_copy(cg.at[slab], cg.at[slab], i, sem_cs, sem_cr) for i in range(SLABS - 1)]
    for copy in coefs:
        copy.start()

    def pass_on(i, reach):
        for step in (reach, FAR - reach):
            pl.semaphore_signal(relay.at[i], inc=1, device_id=(slab, far_peer(step) * NEAR + near), device_id_type=MESH)

    pass_on(0, 2)

    for load in loads[5:]:
        load.wait()
    down = lax.broadcasted_iota(jnp.int32, (HALF, HALF), 0)
    across = lax.broadcasted_iota(jnp.int32, (HALF, HALF), 1)
    regroup = (down == lax.rem(across, 128) * 2 + across // 128).astype(F32).astype(BF16)
    natural = jnp.broadcast_to(low_row[...], (HALF, HALF))
    pick = nn((down == natural).astype(F32).astype(BF16), regroup).astype(BF16)
    lowest = pick[0:1, :].astype(F32)
    for q in range(8):
        wave_own[q] = nn(wave_raw[q], pick).astype(BF16)

    pl.semaphore_wait(relay.at[0], 2)
    pass_on(1, 4)

    for copy in coefs:
        copy.wait()

    gathered = [cg[i].astype(F32) for i in range(SLABS)]
    lhs = jnp.concatenate(
        [gathered[i][f * 8 : (f + 1) * 8] for f in range(3) for i in range(SLABS)], axis=0
    ).astype(BF16)
    first_pair = lax.rem(lax.broadcasted_iota(jnp.int32, (96, 512), 0), 2) == 0
    synth = jnp.where(first_pair, nn(lhs, masked[0]), nn(lhs, masked[1]))
    for b in range(4):
        flat[b * 96 : (b + 1) * 96, :] = synth[:, b * 128 : (b + 1) * 128]
    for g in range(3):
        block = flat[g * 128 : (g + 1) * 128, :].T
        s1[:, :, g * 128 : (g + 1) * 128] = block.reshape(NEAR, FAR, 128).astype(BF16)
    hop1 = near_copies(s1, r1, sem_1s, sem_1r)
    for copy in hop1:
        copy.start()
    r1[near] = s1[near]

    row8 = lax.broadcasted_iota(jnp.int32, (8, PADDED), 0)
    lane8 = lax.broadcasted_iota(jnp.int32, (8, PADDED), 1)
    low8 = jnp.where(lax.rem(row8, 2) == 0, lows[mode * 2], lows[mode * 2 + 1])
    degree = jnp.where(lane8 < ORDERS - low8, low8 + lane8, lane8 - 1).astype(F32)
    degree = degree * (degree + 1.0) * (shell_step * shell_step)
    first_shell = row8 < 4
    for f in range(3):
        diagonal = []
        for s in range(8):
            radius = inner_radius + (s + 0.5) * shell_step
            diagonal.append(degree * (1.0 / (radius * radius)) + (1.0 / diffusion[f] + 2.0))
        leading = [jnp.ones((8, PADDED), F32), diagonal[0]]
        trailing = [jnp.ones((8, PADDED), F32), diagonal[7]]
        for s in range(1, 8):
            leading.append(diagonal[s] * leading[s] - leading[s - 1])
            trailing.append(diagonal[7 - s] * trailing[s] - trailing[s - 1])
        share = 1.0 / leading[8]
        scaled = [value * share for value in leading]

        def entry(i, j):
            return scaled[min(i, j)] * trailing[7 - max(i, j)]

        for i in range(SLABS):
            for j in range(i, SLABS):
                inv[f, 0, i, j] = jnp.where(first_shell, entry(2 * i, 2 * j), entry(2 * i + 1, 2 * j + 1))
                inv[f, 1, i, j] = jnp.where(first_shell, entry(2 * i, 2 * j + 1), entry(2 * i + 1, 2 * j))
                if i != j:
                    inv[f, 0, j, i] = jnp.where(first_shell, entry(2 * i, 2 * j), entry(2 * i + 1, 2 * j + 1))
                    inv[f, 1, j, i] = jnp.where(first_shell, entry(2 * i + 1, 2 * j), entry(2 * i, 2 * j + 1))


    for copy in hop1:
        copy.wait()
    arrived = r1[...].reshape(128, QUARTER).astype(F32)
    for g in range(3):
        mid[g] = arrived[:, g * 128 : (g + 1) * 128]
    for z in range(FAR):
        s2[z] = jnp.concatenate([mid[g, pl.ds(z, NEAR, stride=FAR), :] for g in range(3)], axis=0).astype(BF16)
    pl.semaphore_wait(relay.at[1], 2)
    hop2 = far_copies(s2, r2, sem_2s, sem_2r)
    for copy in hop2:
        copy.start()
    r2[far] = s2[far]

    for copy in hop2:
        copy.wait()
    arrived = r2[...].astype(F32)
    for g in range(3):
        flat[g * 128 : (g + 1) * 128, :] = arrived[:, g * 8 : (g + 1) * 8, :].reshape(128, 128).T

    parts = []
    for q in range(2):
        for c in range(2):
            rows = [
                jnp.concatenate(
                    [flat[pl.ds((h * 2 + q) * 96 + c * 2 + p, 24, stride=4), :] for p in range(2)], axis=1
                )
                for h in range(2)
            ]
            data = jnp.concatenate(rows, axis=0).astype(BF16)
            at = q * 2 + c
            parts.append(nt(data, wave_own[at]) + nt(data, wave_own[4 + at]))
    a, b = parts[0] + parts[2], parts[1] + parts[3]
    c, d = parts[0] - parts[2], parts[1] - parts[3]
    images = (a + b, a - b, c - d, c + d)
    sums = [[], [], [], []]
    for h in range(2):
        for left, right in ((0, 1), (0, 2), (1, 2)):
            u, v = h * 24 + left * 8, h * 24 + right * 8
            p1, p2, p3, p4 = [image[u : u + 8] * image[v : v + 8] for image in images]
            both, across = p1 + p2, p3 + p4
            turn, twist = p1 - p2, p4 - p3
            sums[0].append(both + across)
            sums[1].append(turn + twist)
            sums[2].append(both - across)
            sums[3].append(turn - twist)
    for q in range(2):
        for c in range(2):
            at = q * 2 + c
            value = jnp.concatenate(sums[at], axis=0)
            head = value.astype(BF16)
            tail = (value - head.astype(F32)).astype(BF16)
            answer = nn(head, wave_own[at]) + (nn(tail, wave_own[at]) + nn(head, wave_own[4 + at]))
            if q == 0:
                answer = answer * (0.5 * KAPPA * (1.0 + lowest))
            else:
                answer = answer * (0.5 * KAPPA)
            for h in range(2):
                for p in range(2):
                    flat[pl.ds((h * 2 + q) * 96 + c * 2 + p, 24, stride=4), :] = answer[
                        h * 24 : (h + 1) * 24, p * 128 : (p + 1) * 128
                    ]
    turned = [flat[g * 128 : (g + 1) * 128, :].T.reshape(FAR, NEAR, 128) for g in range(3)]
    s3[...] = jnp.concatenate(turned, axis=1).astype(BF16)
    hop3 = far_copies(s3, r3, sem_3s, sem_3r)
    for copy in hop3:
        copy.start()
    r3[far] = s3[far]
    for copy in hop3:
        copy.wait()
    mid3[...] = r3[...].astype(F32).reshape(FAR * 24, 128)
    for y in range(NEAR):
        s4[y] = jnp.concatenate(
            [mid3[pl.ds(g * 8 + y, FAR, stride=24), :] for g in range(3)], axis=1
        ).astype(BF16)
    hop4 = near_copies(s4, r4, sem_4s, sem_4r)
    for copy in hop4:
        copy.start()
    r4[near] = s4[near]
    for copy in hop4:
        copy.wait()

    arrived = r4[...].reshape(128, QUARTER).astype(F32)
    for g in range(3):
        flat[g * 128 : (g + 1) * 128, :] = arrived[:, g * 128 : (g + 1) * 128].T
    lhs = jnp.concatenate([flat[b * 96 : (b + 1) * 96, :] for b in range(4)], axis=1).astype(BF16)
    first_pair = lax.rem(lax.broadcasted_iota(jnp.int32, (96, PADDED), 0), 2) == 0
    nonlinear = jnp.where(first_pair, nt(lhs, masked[0]), nt(lhs, masked[1]))
    for f in range(3):
        own = st[f * 8 : (f + 1) * 8, :] * (2.0 / diffusion[f])
        drives, swapped = [], []
        for i in range(SLABS):
            start = f * 32 + i * 8
            mine = (slab == i).astype(F32)
            drive = nonlinear[start : start + 8] * coupling[f] + own * mine
            drives.append(drive)
            swapped.append(pltpu.roll(drive, 4, 0))
        for i in range(SLABS):
            value = inv[f, 0, i, 0] * drives[0] + inv[f, 1, i, 0] * swapped[0]
            for j in range(1, SLABS):
                value = value + inv[f, 0, i, j] * drives[j] + inv[f, 1, i, j] * swapped[j]
            send_x[i, f * 8 : (f + 1) * 8, :] = value
    last = [x_copy(send_x.at[x_peer(X_STEPS[i])], recv_x.at[i], i, sem_us, sem_ur) for i in range(SLABS - 1)]
    for copy in last:
        copy.start()
    total[...] = send_x[slab] - st[...]
    for copy in last:
        copy.wait()
    total[...] = total[...] + recv_x[0] + recv_x[1] + recv_x[2]
    for f in range(3):
        for s in range(2):
            for c in range(2):
                for p in range(2):
                    row = f * 8 + s * 4 + c * 2 + p
                    out[p, f, s, c : c + 1, :] = total[row : row + 1, 0:ROWS]


def body(spectral_state, synthesis_table, low_orders, diffusion, coupling):
    low_row = low_orders.reshape(1, HALF)
    vmem = pl.BlockSpec(memory_space=pltpu.VMEM)
    hbm = pl.BlockSpec(memory_space=pltpu.HBM)
    dma = pltpu.SemaphoreType.DMA
    return pl.pallas_call(
        kernel,
        out_shape=pltpu.VMEM(spectral_state.shape, F32),
        in_specs=[hbm] * 7,
        out_specs=vmem,
        scratch_shapes=[
            pltpu.VMEM(spectral_state.shape, F32),
            pltpu.VMEM((ROWS, 2, 128), BF16),
            pltpu.VMEM((2 * ROWS, 128), F32),
            pltpu.VMEM((1, HALF), jnp.int32),
            pltpu.SMEM((HALF,), jnp.int32),
            pltpu.SMEM((3,), F32),
            pltpu.SMEM((3,), F32),
            pltpu.VMEM((8, QUARTER, HALF), BF16),
            pltpu.VMEM((8, QUARTER, HALF), BF16),
            pltpu.VMEM((2, PADDED, 512), BF16),
            pltpu.VMEM((24, PADDED), F32),
            pltpu.VMEM((SLABS, 24, PADDED), BF16),
            pltpu.VMEM((384, 128), F32),
            pltpu.VMEM((NEAR, FAR, 384), BF16),
            pltpu.VMEM((FAR, 24, 128), BF16),
            pltpu.VMEM((NEAR, FAR, 384), BF16),
            pltpu.VMEM((FAR, 24, 128), BF16),
            pltpu.VMEM((FAR, 24, 128), BF16),
            pltpu.VMEM((FAR, 24, 128), BF16),
            pltpu.VMEM((NEAR, FAR, 384), BF16),
            pltpu.VMEM((NEAR, FAR, 384), BF16),
            pltpu.VMEM((3, 128, 128), F32),
            pltpu.VMEM((FAR * 24, 128), F32),
            pltpu.VMEM((3, 2, SLABS, SLABS, 8, PADDED), F32),
            pltpu.VMEM((SLABS, 24, PADDED), F32),
            pltpu.VMEM((SLABS - 1, 24, PADDED), F32),
            pltpu.VMEM((24, PADDED), F32),
            pltpu.SemaphoreType.REGULAR((2,)),
            dma((7,)),
            dma((SLABS - 1,)), dma((SLABS - 1,)),
            dma((NEAR - 1,)), dma((NEAR - 1,)),
            dma((FAR - 1,)), dma((FAR - 1,)),
            dma((FAR - 1,)), dma((FAR - 1,)),
            dma((NEAR - 1,)), dma((NEAR - 1,)),
            dma((SLABS - 1,)), dma((SLABS - 1,)),
        ],
        compiler_params=pltpu.CompilerParams(
            collective_id=0, has_side_effects=True, vmem_limit_bytes=63 * 1024 * 1024
        ),
    )(spectral_state, jnp.transpose(synthesis_table, (1, 0, 2)), low_row, low_orders, diffusion, coupling, jnp.asarray(wave_tables()))


def solution(mesh):
    placed = (P("mode", None, "radial", None, None), P("mode", None, "radial"), P(), P(), P())
    return jax.shard_map(
        body,
        mesh=mesh,
        in_specs=placed,
        out_specs=P("mode", None, "radial", None, None),
        check_vma=False,
    )
```

```python
import math

import jax
import jax.numpy as jnp
import ml_dtypes
import numpy as np
from jax import lax
from jax.experimental import pallas as pl
from jax.experimental.pallas import tpu as pltpu
from jax.sharding import PartitionSpec as P

inner_radius = 0.538
shell_step = 1.0 / 2048.0

ORDERS = 512
HALF = 256
ROWS = 513
PADDED = 640
NLON = 1536
QUARTER = 384
NLAT = 1024
SLABS = 4
NEAR = 8
FAR = 16
X_STEPS = (2, 1, 3)
NEAR_STEPS = ((2, 0), (2, 1), (1, 0), (3, 0), (1, 1), (3, 1), (0, 1))
FAR_STEPS = (8, 7, 9, 6, 10, 5, 11, 4, 12, 3, 13, 2, 14, 1, 15)
GREETED = (2, 14, 1, 15)
KAPPA = 2.0 * math.sqrt(ORDERS * (ORDERS + 1) / (NLAT * NLON))
MESH = pl.DeviceIdType.MESH
F32 = jnp.float32
BF16 = jnp.bfloat16


def wave_tables():
    low = np.arange(HALF)
    even = np.where(low % 2 == 0, low, ORDERS - 1 - low)
    twice = 2 * np.arange(QUARTER)[:, None] + 1
    heads, tails = [], []
    for order in (even, ORDERS - 1 - even):
        weight = np.where(order == 0, 1.0, 2.0)
        angle = (order[None, :] * twice % (2 * NLON)) * (math.pi / NLON)
        for wave in (weight * np.cos(angle), -weight * np.sin(angle)):
            head = wave.astype(ml_dtypes.bfloat16)
            heads.append(head)
            tails.append((wave - head.astype(np.float64)).astype(ml_dtypes.bfloat16))
    return np.stack(heads + tails)


def nn(a, b):
    return lax.dot_general(a, b, (((1,), (0,)), ((), ())), preferred_element_type=F32)


def nt(a, b):
    return lax.dot_general(a, b, (((1,), (1,)), ((), ())), preferred_element_type=F32)


def kernel(
    state_hbm, table_hbm, low_hbm, lows_hbm, diffusion_hbm, coupling_hbm, waves, out,
    state, table, rows, low_row, lows, diffusion, coupling,
    wave_raw, wave_own, masked, st, cg, flat, s1, s2, r1, r2, s3, r3, s4, r4, mid, mid3, inv, kept, send_x, recv_x, total,
    relay, load_sem, sem_cs, sem_cr, sem_1s, sem_1r, sem_2s, sem_2r, sem_3s, sem_3r, sem_4s, sem_4r, sem_us, sem_ur,
):
    slab = lax.axis_index("radial")
    mode = lax.axis_index("mode")
    far = mode // NEAR
    near = lax.rem(mode, NEAR)

    def x_peer(step):
        return lax.rem(slab + step, SLABS)

    def near_peer(step):
        return lax.rem(near // 2 + step[0], 4) * 2 + lax.rem(lax.rem(near, 2) + step[1], 2)

    def far_peer(step):
        return lax.rem(far + step, FAR)

    barrier = pltpu.get_barrier_semaphore()
    for step in GREETED:
        pl.semaphore_signal(barrier, inc=1, device_id=(slab, far_peer(step) * NEAR + near), device_id_type=MESH)
    for step in NEAR_STEPS:
        pl.semaphore_signal(barrier, inc=1, device_id=(slab, far * NEAR + near_peer(step)), device_id_type=MESH)
    for step in X_STEPS:
        pl.semaphore_signal(barrier, inc=1, device_id=(x_peer(step), mode), device_id_type=MESH)

    loads = [
        pltpu.make_async_copy(source, target, load_sem.at[i])
        for i, (source, target) in enumerate(
            (
                (lows_hbm, lows), (diffusion_hbm, diffusion), (coupling_hbm, coupling), (state_hbm, state),
                (table_hbm, table), (low_hbm, low_row), (waves, wave_raw),
            )
        )
    ]
    for load in loads:
        load.start()

    st[...] = jnp.zeros_like(st)
    for load in loads[:4]:
        load.wait()
    for f in range(3):
        for s in range(2):
            for c in range(2):
                for p in range(2):
                    row = f * 8 + s * 4 + c * 2 + p
                    st[row : row + 1, 0:ROWS] = state[p, f, s, c : c + 1, :]
    cg[slab] = st[...].astype(BF16)

    def x_copy(source, target, i, send, recv):
        return pltpu.make_async_remote_copy(
            src_ref=source, dst_ref=target, send_sem=send.at[i], recv_sem=recv.at[i],
            device_id=(x_peer(X_STEPS[i]), mode), device_id_type=MESH,
        )

    def near_copies(source, target, send, recv):
        return [
            pltpu.make_async_remote_copy(
                src_ref=source.at[near_peer(step)], dst_ref=target.at[near], send_sem=send.at[i], recv_sem=recv.at[i],
                device_id=(slab, far * NEAR + near_peer(step)), device_id_type=MESH,
            )
            for i, step in enumerate(NEAR_STEPS)
        ]

    def far_copies(source, target, send, recv):
        return [
            pltpu.make_async_remote_copy(
                src_ref=source.at[far_peer(step)], dst_ref=target.at[far], send_sem=send.at[i], recv_sem=recv.at[i],
                device_id=(slab, far_peer(step) * NEAR + near), device_id_type=MESH,
            )
            for i, step in enumerate(FAR_STEPS)
        ]

    loads[4].wait()
    rows[...] = table[...].astype(F32).reshape(2 * ROWS, 128)
    for p in range(2):
        low = lows[mode * 2 + p]
        low_even = lax.rem(low, 2) == 0
        for start, size in ((0, 512), (512, 128)):
            row = lax.broadcasted_iota(jnp.int32, (size, 128), 0) + start
            if start == 0:
                values = rows[pl.ds(p, 512, stride=2), :]
            else:
                last = rows[1024 + p : 1025 + p, :]
                values = jnp.where(row == 512, jnp.broadcast_to(last, (128, 128)), 0.0)
            in_lower = row < ORDERS - low
            even_order = in_lower == low_even
            odd_sum = jnp.where(in_lower, lax.rem(row, 2), lax.rem(row + low, 2))
            sign = 1.0 - 2.0 * odd_sum.astype(F32)
            for q in range(2):
                north = jnp.where(even_order == (q == 0), values, 0.0)
                masked[p, start : start + size, q * 128 : (q + 1) * 128] = north.astype(BF16)
                masked[p, start : start + size, (2 + q) * 128 : (3 + q) * 128] = (north * sign).astype(BF16)

    pl.semaphore_wait(barrier, SLABS - 1 + NEAR - 1 + len(GREETED))

    coefs = [x_copy(cg.at[slab], cg.at[slab], i, sem_cs, sem_cr) for i in range(SLABS - 1)]
    for copy in coefs:
        copy.start()

    def pass_on(i, reach):
        for step in (reach, FAR - reach):
            pl.semaphore_signal(relay.at[i], inc=1, device_id=(slab, far_peer(step) * NEAR + near), device_id_type=MESH)

    pass_on(0, 2)

    pl.semaphore_wait(relay.at[0], 2)
    pass_on(1, 4)

    for copy in coefs:
        copy.wait()

    gathered = [cg[i].astype(F32) for i in range(SLABS)]
    lhs = jnp.concatenate(
        [gathered[i][f * 8 : (f + 1) * 8] for f in range(3) for i in range(SLABS)], axis=0
    ).astype(BF16)
    first_pair = lax.rem(lax.broadcasted_iota(jnp.int32, (96, 512), 0), 2) == 0
    synth = jnp.where(first_pair, nn(lhs, masked[0]), nn(lhs, masked[1]))
    for b in range(4):
        flat[b * 96 : (b + 1) * 96, :] = synth[:, b * 128 : (b + 1) * 128]
    for g in range(3):
        block = flat[g * 128 : (g + 1) * 128, :].T
        s1[:, :, g * 128 : (g + 1) * 128] = block.reshape(NEAR, FAR, 128).astype(BF16)
    hop1 = near_copies(s1, r1, sem_1s, sem_1r)
    for copy in hop1:
        copy.start()
    r1[near] = s1[near]

    for copy in hop1:
        copy.wait()
    arrived = r1[...].reshape(128, QUARTER).astype(F32)
    for g in range(3):
        mid[g] = arrived[:, g * 128 : (g + 1) * 128]
    for z in range(FAR):
        s2[z] = jnp.concatenate([mid[g, pl.ds(z, NEAR, stride=FAR), :] for g in range(3)], axis=0).astype(BF16)
    pl.semaphore_wait(relay.at[1], 2)
    hop2 = far_copies(s2, r2, sem_2s, sem_2r)
    for copy in hop2:
        copy.start()
    r2[far] = s2[far]

    for load in loads[5:]:
        load.wait()
    down = lax.broadcasted_iota(jnp.int32, (HALF, HALF), 0)
    across = lax.broadcasted_iota(jnp.int32, (HALF, HALF), 1)
    regroup = (down == lax.rem(across, 128) * 2 + across // 128).astype(F32).astype(BF16)
    natural = jnp.broadcast_to(low_row[...], (HALF, HALF))
    pick = nn((down == natural).astype(F32).astype(BF16), regroup).astype(BF16)
    lowest = pick[0:1, :].astype(F32)
    for q in range(8):
        wave_own[q] = nn(wave_raw[q], pick).astype(BF16)


    for copy in hop2:
        copy.wait()
    arrived = r2[...].astype(F32)
    for g in range(3):
        flat[g * 128 : (g + 1) * 128, :] = arrived[:, g * 8 : (g + 1) * 8, :].reshape(128, 128).T

    parts = []
    for q in range(2):
        for c in range(2):
            rows = [
                jnp.concatenate(
                    [flat[pl.ds((h * 2 + q) * 96 + c * 2 + p, 24, stride=4), :] for p in range(2)], axis=1
                )
                for h in range(2)
            ]
            data = jnp.concatenate(rows, axis=0).astype(BF16)
            at = q * 2 + c
            parts.append(nt(data, wave_own[at]) + nt(data, wave_own[4 + at]))
    a, b = parts[0] + parts[2], parts[1] + parts[3]
    c, d = parts[0] - parts[2], parts[1] - parts[3]
    images = (a + b, a - b, c - d, c + d)
    sums = [[], [], [], []]
    for h in range(2):
        for left, right in ((0, 1), (0, 2), (1, 2)):
            u, v = h * 24 + left * 8, h * 24 + right * 8
            p1, p2, p3, p4 = [image[u : u + 8] * image[v : v + 8] for image in images]
            both, across = p1 + p2, p3 + p4
            turn, twist = p1 - p2, p4 - p3
            sums[0].append(both + across)
            sums[1].append(turn + twist)
            sums[2].append(both - across)
            sums[3].append(turn - twist)
    for q in range(2):
        for c in range(2):
            at = q * 2 + c
            value = jnp.concatenate(sums[at], axis=0)
            head = value.astype(BF16)
            tail = (value - head.astype(F32)).astype(BF16)
            answer = nn(head, wave_own[at]) + (nn(tail, wave_own[at]) + nn(head, wave_own[4 + at]))
            if q == 0:
                answer = answer * (0.5 * KAPPA * (1.0 + lowest))
            else:
                answer = answer * (0.5 * KAPPA)
            for h in range(2):
                for p in range(2):
                    flat[pl.ds((h * 2 + q) * 96 + c * 2 + p, 24, stride=4), :] = answer[
                        h * 24 : (h + 1) * 24, p * 128 : (p + 1) * 128
                    ]
    turned = [flat[g * 128 : (g + 1) * 128, :].T.reshape(FAR, NEAR, 128) for g in range(3)]
    s3[...] = jnp.concatenate(turned, axis=1).astype(BF16)
    hop3 = far_copies(s3, r3, sem_3s, sem_3r)
    for copy in hop3:
        copy.start()
    r3[far] = s3[far]

    row8 = lax.broadcasted_iota(jnp.int32, (8, PADDED), 0)
    lane8 = lax.broadcasted_iota(jnp.int32, (8, PADDED), 1)
    low8 = jnp.where(lax.rem(row8, 2) == 0, lows[mode * 2], lows[mode * 2 + 1])
    degree = jnp.where(lane8 < ORDERS - low8, low8 + lane8, lane8 - 1).astype(F32)
    degree = degree * (degree + 1.0) * (shell_step * shell_step)
    first_shell = row8 < 4
    for f in range(3):
        diagonal = []
        for s in range(8):
            radius = inner_radius + (s + 0.5) * shell_step
            diagonal.append(degree * (1.0 / (radius * radius)) + (1.0 / diffusion[f] + 2.0))
        leading = [jnp.ones((8, PADDED), F32), diagonal[0]]
        trailing = [jnp.ones((8, PADDED), F32), diagonal[7]]
        for s in range(1, 8):
            leading.append(diagonal[s] * leading[s] - leading[s - 1])
            trailing.append(diagonal[7 - s] * trailing[s] - trailing[s - 1])
        share = 1.0 / leading[8]
        scaled = [value * share for value in leading]

        def entry(i, j):
            return scaled[min(i, j)] * trailing[7 - max(i, j)]

        for i in range(SLABS):
            for j in range(i, SLABS):
                inv[f, 0, i, j] = jnp.where(first_shell, entry(2 * i, 2 * j), entry(2 * i + 1, 2 * j + 1))
                inv[f, 1, i, j] = jnp.where(first_shell, entry(2 * i, 2 * j + 1), entry(2 * i + 1, 2 * j))
                if i != j:
                    inv[f, 0, j, i] = jnp.where(first_shell, entry(2 * i, 2 * j), entry(2 * i + 1, 2 * j + 1))
                    inv[f, 1, j, i] = jnp.where(first_shell, entry(2 * i + 1, 2 * j), entry(2 * i, 2 * j + 1))

    for copy in hop3:
        copy.wait()
    mid3[...] = r3[...].astype(F32).reshape(FAR * 24, 128)
    for y in range(NEAR):
        s4[y] = jnp.concatenate(
            [mid3[pl.ds(g * 8 + y, FAR, stride=24), :] for g in range(3)], axis=1
        ).astype(BF16)
    hop4 = near_copies(s4, r4, sem_4s, sem_4r)
    for copy in hop4:
        copy.start()
    r4[near] = s4[near]
    for copy in hop4:
        copy.wait()

    arrived = r4[...].reshape(128, QUARTER).astype(F32)
    for g in range(3):
        flat[g * 128 : (g + 1) * 128, :] = arrived[:, g * 128 : (g + 1) * 128].T
    lhs = jnp.concatenate([flat[b * 96 : (b + 1) * 96, :] for b in range(4)], axis=1).astype(BF16)
    first_pair = lax.rem(lax.broadcasted_iota(jnp.int32, (96, PADDED), 0), 2) == 0
    nonlinear = jnp.where(first_pair, nt(lhs, masked[0]), nt(lhs, masked[1]))
    values = [[] for _ in range(SLABS)]
    for f in range(3):
        own = st[f * 8 : (f + 1) * 8, :] * (2.0 / diffusion[f])
        drives, swapped = [], []
        for i in range(SLABS):
            start = f * 32 + i * 8
            mine = (slab == i).astype(F32)
            drive = nonlinear[start : start + 8] * coupling[f] + own * mine
            drives.append(drive)
            swapped.append(pltpu.roll(drive, 4, 0))
        for i in range(SLABS):
            value = inv[f, 0, i, 0] * drives[0] + inv[f, 1, i, 0] * swapped[0]
            for j in range(1, SLABS):
                value = value + inv[f, 0, i, j] * drives[j] + inv[f, 1, i, j] * swapped[j]
            values[i].append(value)
    for i in range(SLABS):
        whole = jnp.concatenate(values[i], axis=0)
        kept[i] = whole
        send_x[i] = whole.astype(BF16)
    last = [x_copy(send_x.at[x_peer(X_STEPS[i])], recv_x.at[i], i, sem_us, sem_ur) for i in range(SLABS - 1)]
    for copy in last:
        copy.start()
    total[...] = kept[slab] - st[...]
    for copy in last:
        copy.wait()
    total[...] = total[...] + recv_x[0].astype(F32) + recv_x[1].astype(F32) + recv_x[2].astype(F32)
    for f in range(3):
        for s in range(2):
            for c in range(2):
                for p in range(2):
                    row = f * 8 + s * 4 + c * 2 + p
                    out[p, f, s, c : c + 1, :] = total[row : row + 1, 0:ROWS]


def body(spectral_state, synthesis_table, low_orders, diffusion, coupling):
    low_row = low_orders.reshape(1, HALF)
    vmem = pl.BlockSpec(memory_space=pltpu.VMEM)
    hbm = pl.BlockSpec(memory_space=pltpu.HBM)
    dma = pltpu.SemaphoreType.DMA
    return pl.pallas_call(
        kernel,
        out_shape=pltpu.VMEM(spectral_state.shape, F32),
        in_specs=[hbm] * 7,
        out_specs=vmem,
        scratch_shapes=[
            pltpu.VMEM(spectral_state.shape, F32),
            pltpu.VMEM((ROWS, 2, 128), BF16),
            pltpu.VMEM((2 * ROWS, 128), F32),
            pltpu.VMEM((1, HALF), jnp.int32),
            pltpu.SMEM((HALF,), jnp.int32),
            pltpu.SMEM((3,), F32),
            pltpu.SMEM((3,), F32),
            pltpu.VMEM((8, QUARTER, HALF), BF16),
            pltpu.VMEM((8, QUARTER, HALF), BF16),
            pltpu.VMEM((2, PADDED, 512), BF16),
            pltpu.VMEM((24, PADDED), F32),
            pltpu.VMEM((SLABS, 24, PADDED), BF16),
            pltpu.VMEM((384, 128), F32),
            pltpu.VMEM((NEAR, FAR, 384), BF16),
            pltpu.VMEM((FAR, 24, 128), BF16),
            pltpu.VMEM((NEAR, FAR, 384), BF16),
            pltpu.VMEM((FAR, 24, 128), BF16),
            pltpu.VMEM((FAR, 24, 128), BF16),
            pltpu.VMEM((FAR, 24, 128), BF16),
            pltpu.VMEM((NEAR, FAR, 384), BF16),
            pltpu.VMEM((NEAR, FAR, 384), BF16),
            pltpu.VMEM((3, 128, 128), F32),
            pltpu.VMEM((FAR * 24, 128), F32),
            pltpu.VMEM((3, 2, SLABS, SLABS, 8, PADDED), F32),
            pltpu.VMEM((SLABS, 24, PADDED), F32),
            pltpu.VMEM((SLABS, 24, PADDED), BF16),
            pltpu.VMEM((SLABS - 1, 24, PADDED), BF16),
            pltpu.VMEM((24, PADDED), F32),
            pltpu.SemaphoreType.REGULAR((2,)),
            dma((7,)),
            dma((SLABS - 1,)), dma((SLABS - 1,)),
            dma((NEAR - 1,)), dma((NEAR - 1,)),
            dma((FAR - 1,)), dma((FAR - 1,)),
            dma((FAR - 1,)), dma((FAR - 1,)),
            dma((NEAR - 1,)), dma((NEAR - 1,)),
            dma((SLABS - 1,)), dma((SLABS - 1,)),
        ],
        compiler_params=pltpu.CompilerParams(
            collective_id=0, has_side_effects=True, vmem_limit_bytes=63 * 1024 * 1024
        ),
    )(spectral_state, jnp.transpose(synthesis_table, (1, 0, 2)), low_row, low_orders, diffusion, coupling, jnp.asarray(wave_tables()))


def solution(mesh):
    placed = (P("mode", None, "radial", None, None), P("mode", None, "radial"), P(), P(), P())
    return jax.shard_map(
        body,
        mesh=mesh,
        in_specs=placed,
        out_specs=P("mode", None, "radial", None, None),
        check_vma=False,
    )
```

```python
import math

import jax
import jax.numpy as jnp
import ml_dtypes
import numpy as np
from jax import lax
from jax.experimental import pallas as pl
from jax.experimental.pallas import tpu as pltpu
from jax.sharding import PartitionSpec as P

inner_radius = 0.538
shell_step = 1.0 / 2048.0

ORDERS = 512
HALF = 256
ROWS = 513
PADDED = 640
NLON = 1536
QUARTER = 384
NLAT = 1024
SLABS = 4
NEAR = 8
FAR = 16
X_STEPS = (2, 1, 3)
NEAR_STEPS = ((2, 0), (2, 1), (1, 0), (3, 0), (1, 1), (3, 1), (0, 1))
FAR_STEPS = (8, 7, 9, 6, 10, 5, 11, 4, 12, 3, 13, 2, 14, 1, 15)
ALL_STEPS = sorted(
    ((z, y, c) for z in range(FAR) for y in range(4) for c in range(2) if z or y or c),
    key=lambda step: (-min(step[0], FAR - step[0]) - min(step[1], 4 - step[1]), step),
)
GREETED = (2, 14, 1, 15)
KAPPA = 2.0 * math.sqrt(ORDERS * (ORDERS + 1) / (NLAT * NLON))
MESH = pl.DeviceIdType.MESH
F32 = jnp.float32
BF16 = jnp.bfloat16


def wave_tables():
    low = np.arange(HALF)
    even = np.where(low % 2 == 0, low, ORDERS - 1 - low)
    twice = 2 * np.arange(QUARTER)[:, None] + 1
    heads, tails = [], []
    for order in (even, ORDERS - 1 - even):
        weight = np.where(order == 0, 1.0, 2.0)
        angle = (order[None, :] * twice % (2 * NLON)) * (math.pi / NLON)
        for wave in (weight * np.cos(angle), -weight * np.sin(angle)):
            head = wave.astype(ml_dtypes.bfloat16)
            heads.append(head)
            tails.append((wave - head.astype(np.float64)).astype(ml_dtypes.bfloat16))
    return np.stack(heads + tails)


def nn(a, b):
    return lax.dot_general(a, b, (((1,), (0,)), ((), ())), preferred_element_type=F32)


def nt(a, b):
    return lax.dot_general(a, b, (((1,), (1,)), ((), ())), preferred_element_type=F32)


def kernel(
    state_hbm, table_hbm, low_hbm, lows_hbm, diffusion_hbm, coupling_hbm, waves, out,
    state, table, rows, low_row, lows, diffusion, coupling,
    wave_raw, wave_own, masked, st, cg, flat, s1, s2, r1, r2, s3, r3, mid, mid4, inv, send_x, recv_x, total,
    relay, load_sem, sem_cs, sem_cr, sem_1s, sem_1r, sem_2s, sem_2r, sem_3s, sem_3r, sem_us, sem_ur,
):
    slab = lax.axis_index("radial")
    mode = lax.axis_index("mode")
    far = mode // NEAR
    near = lax.rem(mode, NEAR)

    def x_peer(step):
        return lax.rem(slab + step, SLABS)

    def near_peer(step):
        return lax.rem(near // 2 + step[0], 4) * 2 + lax.rem(lax.rem(near, 2) + step[1], 2)

    def far_peer(step):
        return lax.rem(far + step, FAR)

    barrier = pltpu.get_barrier_semaphore()
    for step in GREETED:
        pl.semaphore_signal(barrier, inc=1, device_id=(slab, far_peer(step) * NEAR + near), device_id_type=MESH)
    for step in NEAR_STEPS:
        pl.semaphore_signal(barrier, inc=1, device_id=(slab, far * NEAR + near_peer(step)), device_id_type=MESH)
    for step in X_STEPS:
        pl.semaphore_signal(barrier, inc=1, device_id=(x_peer(step), mode), device_id_type=MESH)

    loads = [
        pltpu.make_async_copy(source, target, load_sem.at[i])
        for i, (source, target) in enumerate(
            (
                (lows_hbm, lows), (diffusion_hbm, diffusion), (coupling_hbm, coupling), (state_hbm, state),
                (table_hbm, table), (low_hbm, low_row), (waves, wave_raw),
            )
        )
    ]
    for load in loads:
        load.start()

    st[...] = jnp.zeros_like(st)
    mid4[...] = jnp.zeros_like(mid4)
    for load in loads[:4]:
        load.wait()
    for f in range(3):
        for s in range(2):
            for c in range(2):
                for p in range(2):
                    row = f * 8 + s * 4 + c * 2 + p
                    st[row : row + 1, 0:ROWS] = state[p, f, s, c : c + 1, :]
    cg[slab] = st[...].astype(BF16)

    def x_copy(source, target, i, send, recv):
        return pltpu.make_async_remote_copy(
            src_ref=source, dst_ref=target, send_sem=send.at[i], recv_sem=recv.at[i],
            device_id=(x_peer(X_STEPS[i]), mode), device_id_type=MESH,
        )

    def near_copies(source, target, send, recv):
        return [
            pltpu.make_async_remote_copy(
                src_ref=source.at[near_peer(step)], dst_ref=target.at[near], send_sem=send.at[i], recv_sem=recv.at[i],
                device_id=(slab, far * NEAR + near_peer(step)), device_id_type=MESH,
            )
            for i, step in enumerate(NEAR_STEPS)
        ]

    def far_copies(source, target, send, recv):
        return [
            pltpu.make_async_remote_copy(
                src_ref=source.at[far_peer(step)], dst_ref=target.at[far], send_sem=send.at[i], recv_sem=recv.at[i],
                device_id=(slab, far_peer(step) * NEAR + near), device_id_type=MESH,
            )
            for i, step in enumerate(FAR_STEPS)
        ]

    loads[4].wait()
    rows[...] = table[...].astype(F32).reshape(2 * ROWS, 128)
    for p in range(2):
        low = lows[mode * 2 + p]
        low_even = lax.rem(low, 2) == 0
        for start, size in ((0, 512), (512, 128)):
            row = lax.broadcasted_iota(jnp.int32, (size, 128), 0) + start
            if start == 0:
                values = rows[pl.ds(p, 512, stride=2), :]
            else:
                last = rows[1024 + p : 1025 + p, :]
                values = jnp.where(row == 512, jnp.broadcast_to(last, (128, 128)), 0.0)
            in_lower = row < ORDERS - low
            even_order = in_lower == low_even
            odd_sum = jnp.where(in_lower, lax.rem(row, 2), lax.rem(row + low, 2))
            sign = 1.0 - 2.0 * odd_sum.astype(F32)
            for q in range(2):
                north = jnp.where(even_order == (q == 0), values, 0.0)
                masked[p, start : start + size, q * 128 : (q + 1) * 128] = north.astype(BF16)
                masked[p, start : start + size, (2 + q) * 128 : (3 + q) * 128] = (north * sign).astype(BF16)

    pl.semaphore_wait(barrier, SLABS - 1 + NEAR - 1 + len(GREETED))

    coefs = [x_copy(cg.at[slab], cg.at[slab], i, sem_cs, sem_cr) for i in range(SLABS - 1)]
    for copy in coefs:
        copy.start()

    def pass_on(i, reach):
        for step in (reach, FAR - reach):
            pl.semaphore_signal(relay.at[i], inc=1, device_id=(slab, far_peer(step) * NEAR + near), device_id_type=MESH)

    pass_on(0, 2)

    pl.semaphore_wait(relay.at[0], 2)
    pass_on(1, 4)

    for copy in coefs:
        copy.wait()

    gathered = [cg[i].astype(F32) for i in range(SLABS)]
    lhs = jnp.concatenate(
        [gathered[i][f * 8 : (f + 1) * 8] for f in range(3) for i in range(SLABS)], axis=0
    ).astype(BF16)
    first_pair = lax.rem(lax.broadcasted_iota(jnp.int32, (96, 512), 0), 2) == 0
    synth = jnp.where(first_pair, nn(lhs, masked[0]), nn(lhs, masked[1]))
    for b in range(4):
        flat[b * 96 : (b + 1) * 96, :] = synth[:, b * 128 : (b + 1) * 128]
    for g in range(3):
        block = flat[g * 128 : (g + 1) * 128, :].T
        s1[:, :, g * 128 : (g + 1) * 128] = block.reshape(NEAR, FAR, 128).astype(BF16)
    hop1 = near_copies(s1, r1, sem_1s, sem_1r)
    for copy in hop1:
        copy.start()
    r1[near] = s1[near]

    for copy in hop1:
        copy.wait()
    arrived = r1[...].reshape(128, QUARTER).astype(F32)
    for g in range(3):
        mid[g] = arrived[:, g * 128 : (g + 1) * 128]
    for z in range(FAR):
        s2[z] = jnp.concatenate([mid[g, pl.ds(z, NEAR, stride=FAR), :] for g in range(3)], axis=0).astype(BF16)
    pl.semaphore_wait(relay.at[1], 2)
    hop2 = far_copies(s2, r2, sem_2s, sem_2r)
    for copy in hop2:
        copy.start()
    r2[far] = s2[far]

    for load in loads[5:]:
        load.wait()
    down = lax.broadcasted_iota(jnp.int32, (HALF, HALF), 0)
    across = lax.broadcasted_iota(jnp.int32, (HALF, HALF), 1)
    regroup = (down == lax.rem(across, 128) * 2 + across // 128).astype(F32).astype(BF16)
    natural = jnp.broadcast_to(low_row[...], (HALF, HALF))
    pick = nn((down == natural).astype(F32).astype(BF16), regroup).astype(BF16)
    lowest = pick[0:1, :].astype(F32)
    for q in range(8):
        wave_own[q] = nn(wave_raw[q], pick).astype(BF16)


    for copy in hop2:
        copy.wait()
    arrived = r2[...].astype(F32)
    for g in range(3):
        flat[g * 128 : (g + 1) * 128, :] = arrived[:, g * 8 : (g + 1) * 8, :].reshape(128, 128).T

    parts = []
    for q in range(2):
        for c in range(2):
            rows = [
                jnp.concatenate(
                    [flat[pl.ds((h * 2 + q) * 96 + c * 2 + p, 24, stride=4), :] for p in range(2)], axis=1
                )
                for h in range(2)
            ]
            data = jnp.concatenate(rows, axis=0).astype(BF16)
            at = q * 2 + c
            parts.append(nt(data, wave_own[at]) + nt(data, wave_own[4 + at]))
    a, b = parts[0] + parts[2], parts[1] + parts[3]
    c, d = parts[0] - parts[2], parts[1] - parts[3]
    images = (a + b, a - b, c - d, c + d)
    sums = [[], [], [], []]
    for h in range(2):
        for left, right in ((0, 1), (0, 2), (1, 2)):
            u, v = h * 24 + left * 8, h * 24 + right * 8
            p1, p2, p3, p4 = [image[u : u + 8] * image[v : v + 8] for image in images]
            both, across = p1 + p2, p3 + p4
            turn, twist = p1 - p2, p4 - p3
            sums[0].append(both + across)
            sums[1].append(turn + twist)
            sums[2].append(both - across)
            sums[3].append(turn - twist)
    for q in range(2):
        for c in range(2):
            at = q * 2 + c
            value = jnp.concatenate(sums[at], axis=0)
            head = value.astype(BF16)
            tail = (value - head.astype(F32)).astype(BF16)
            answer = nn(head, wave_own[at]) + (nn(tail, wave_own[at]) + nn(head, wave_own[4 + at]))
            if q == 0:
                answer = answer * (0.5 * KAPPA * (1.0 + lowest))
            else:
                answer = answer * (0.5 * KAPPA)
            for h in range(2):
                for p in range(2):
                    flat[pl.ds((h * 2 + q) * 96 + c * 2 + p, 24, stride=4), :] = answer[
                        h * 24 : (h + 1) * 24, p * 128 : (p + 1) * 128
                    ]
    for g in range(3):
        mid4[pl.ds(g, 128, stride=4), :] = flat[g * 128 : (g + 1) * 128, :].T
    s3[...] = mid4[...].reshape(128, 4, 128).astype(BF16)
    for z, y, c in ALL_STEPS:
        peer = far_peer(z) * NEAR + near_peer((y, c))
        pltpu.make_async_remote_copy(
            src_ref=s3.at[peer], dst_ref=r3.at[mode], send_sem=sem_3s.at[0], recv_sem=sem_3r.at[0],
            device_id=(slab, peer), device_id_type=MESH,
        ).start()
    r3[mode] = s3[mode]

    row8 = lax.broadcasted_iota(jnp.int32, (8, PADDED), 0)
    lane8 = lax.broadcasted_iota(jnp.int32, (8, PADDED), 1)
    low8 = jnp.where(lax.rem(row8, 2) == 0, lows[mode * 2], lows[mode * 2 + 1])
    degree = jnp.where(lane8 < ORDERS - low8, low8 + lane8, lane8 - 1).astype(F32)
    degree = degree * (degree + 1.0) * (shell_step * shell_step)
    first_shell = row8 < 4
    for f in range(3):
        diagonal = []
        for s in range(8):
            radius = inner_radius + (s + 0.5) * shell_step
            diagonal.append(degree * (1.0 / (radius * radius)) + (1.0 / diffusion[f] + 2.0))
        leading = [jnp.ones((8, PADDED), F32), diagonal[0]]
        trailing = [jnp.ones((8, PADDED), F32), diagonal[7]]
        for s in range(1, 8):
            leading.append(diagonal[s] * leading[s] - leading[s - 1])
            trailing.append(diagonal[7 - s] * trailing[s] - trailing[s - 1])
        share = 1.0 / leading[8]
        scaled = [value * share for value in leading]

        def entry(i, j):
            return scaled[min(i, j)] * trailing[7 - max(i, j)]

        for i in range(SLABS):
            for j in range(i, SLABS):
                inv[f, 0, i, j] = jnp.where(first_shell, entry(2 * i, 2 * j), entry(2 * i + 1, 2 * j + 1))
                inv[f, 1, i, j] = jnp.where(first_shell, entry(2 * i, 2 * j + 1), entry(2 * i + 1, 2 * j))
                if i != j:
                    inv[f, 0, j, i] = jnp.where(first_shell, entry(2 * i, 2 * j), entry(2 * i + 1, 2 * j + 1))
                    inv[f, 1, j, i] = jnp.where(first_shell, entry(2 * i + 1, 2 * j), entry(2 * i, 2 * j + 1))

    others = len(ALL_STEPS)
    pltpu.make_async_copy(r3.at[0:others], r3.at[0:others], sem_3r.at[0]).wait()
    pltpu.make_async_copy(s3.at[0:others], s3.at[0:others], sem_3s.at[0]).wait()

    mid4[...] = r3[...].astype(F32).reshape(512, 128)
    for g in range(3):
        flat[g * 128 : (g + 1) * 128, :] = jnp.concatenate(
            [mid4[pl.ds(y * 4 + g, FAR, stride=32), :] for y in range(NEAR)], axis=0
        ).T
    lhs = jnp.concatenate([flat[b * 96 : (b + 1) * 96, :] for b in range(4)], axis=1).astype(BF16)
    first_pair = lax.rem(lax.broadcasted_iota(jnp.int32, (96, PADDED), 0), 2) == 0
    nonlinear = jnp.where(first_pair, nt(lhs, masked[0]), nt(lhs, masked[1]))
    for f in range(3):
        own = st[f * 8 : (f + 1) * 8, :] * (2.0 / diffusion[f])
        drives, swapped = [], []
        for i in range(SLABS):
            start = f * 32 + i * 8
            mine = (slab == i).astype(F32)
            drive = nonlinear[start : start + 8] * coupling[f] + own * mine
            drives.append(drive)
            swapped.append(pltpu.roll(drive, 4, 0))
        for i in range(SLABS):
            value = inv[f, 0, i, 0] * drives[0] + inv[f, 1, i, 0] * swapped[0]
            for j in range(1, SLABS):
                value = value + inv[f, 0, i, j] * drives[j] + inv[f, 1, i, j] * swapped[j]
            send_x[i, f * 8 : (f + 1) * 8, :] = value
    last = [x_copy(send_x.at[x_peer(X_STEPS[i])], recv_x.at[i], i, sem_us, sem_ur) for i in range(SLABS - 1)]
    for copy in last:
        copy.start()
    total[...] = send_x[slab] - st[...]
    for copy in last:
        copy.wait()
    total[...] = total[...] + recv_x[0] + recv_x[1] + recv_x[2]
    for f in range(3):
        for s in range(2):
            for c in range(2):
                for p in range(2):
                    row = f * 8 + s * 4 + c * 2 + p
                    out[p, f, s, c : c + 1, :] = total[row : row + 1, 0:ROWS]


def body(spectral_state, synthesis_table, low_orders, diffusion, coupling):
    low_row = low_orders.reshape(1, HALF)
    vmem = pl.BlockSpec(memory_space=pltpu.VMEM)
    hbm = pl.BlockSpec(memory_space=pltpu.HBM)
    dma = pltpu.SemaphoreType.DMA
    return pl.pallas_call(
        kernel,
        out_shape=pltpu.VMEM(spectral_state.shape, F32),
        in_specs=[hbm] * 7,
        out_specs=vmem,
        scratch_shapes=[
            pltpu.VMEM(spectral_state.shape, F32),
            pltpu.VMEM((ROWS, 2, 128), BF16),
            pltpu.VMEM((2 * ROWS, 128), F32),
            pltpu.VMEM((1, HALF), jnp.int32),
            pltpu.SMEM((HALF,), jnp.int32),
            pltpu.SMEM((3,), F32),
            pltpu.SMEM((3,), F32),
            pltpu.VMEM((8, QUARTER, HALF), BF16),
            pltpu.VMEM((8, QUARTER, HALF), BF16),
            pltpu.VMEM((2, PADDED, 512), BF16),
            pltpu.VMEM((24, PADDED), F32),
            pltpu.VMEM((SLABS, 24, PADDED), BF16),
            pltpu.VMEM((384, 128), F32),
            pltpu.VMEM((NEAR, FAR, 384), BF16),
            pltpu.VMEM((FAR, 24, 128), BF16),
            pltpu.VMEM((NEAR, FAR, 384), BF16),
            pltpu.VMEM((FAR, 24, 128), BF16),
            pltpu.VMEM((128, 4, 128), BF16),
            pltpu.VMEM((128, 4, 128), BF16),
            pltpu.VMEM((3, 128, 128), F32),
            pltpu.VMEM((512, 128), F32),
            pltpu.VMEM((3, 2, SLABS, SLABS, 8, PADDED), F32),
            pltpu.VMEM((SLABS, 24, PADDED), F32),
            pltpu.VMEM((SLABS - 1, 24, PADDED), F32),
            pltpu.VMEM((24, PADDED), F32),
            pltpu.SemaphoreType.REGULAR((2,)),
            dma((7,)),
            dma((SLABS - 1,)), dma((SLABS - 1,)),
            dma((NEAR - 1,)), dma((NEAR - 1,)),
            dma((FAR - 1,)), dma((FAR - 1,)),
            dma((1,)), dma((1,)),
            dma((SLABS - 1,)), dma((SLABS - 1,)),
        ],
        compiler_params=pltpu.CompilerParams(
            collective_id=0, has_side_effects=True, vmem_limit_bytes=63 * 1024 * 1024
        ),
    )(spectral_state, jnp.transpose(synthesis_table, (1, 0, 2)), low_row, low_orders, diffusion, coupling, jnp.asarray(wave_tables()))


def solution(mesh):
    placed = (P("mode", None, "radial", None, None), P("mode", None, "radial"), P(), P(), P())
    return jax.shard_map(
        body,
        mesh=mesh,
        in_specs=placed,
        out_specs=P("mode", None, "radial", None, None),
        check_vma=False,
    )
```

```python
import math

import jax
import jax.numpy as jnp
import ml_dtypes
import numpy as np
from jax import lax
from jax.experimental import pallas as pl
from jax.experimental.pallas import tpu as pltpu
from jax.sharding import PartitionSpec as P

inner_radius = 0.538
shell_step = 1.0 / 2048.0

ORDERS = 512
HALF = 256
ROWS = 513
PADDED = 640
NLON = 1536
QUARTER = 384
NLAT = 1024
SLABS = 4
NEAR = 8
FAR = 16
X_STEPS = (2, 1, 3)
NEAR_STEPS = ((2, 0), (2, 1), (1, 0), (3, 0), (1, 1), (3, 1), (0, 1))
FAR_STEPS = (8, 7, 9, 6, 10, 5, 11, 4, 12, 3, 13, 2, 14, 1, 15)
ALL_STEPS = sorted(
    ((z, y, c) for z in range(FAR) for y in range(4) for c in range(2) if z or y or c),
    key=lambda step: (-min(step[0], FAR - step[0]) - min(step[1], 4 - step[1]), step[::-1]),
)
GREETED = (2, 14, 1, 15)
KAPPA = 2.0 * math.sqrt(ORDERS * (ORDERS + 1) / (NLAT * NLON))
MESH = pl.DeviceIdType.MESH
F32 = jnp.float32
BF16 = jnp.bfloat16


def wave_tables():
    low = np.arange(HALF)
    even = np.where(low % 2 == 0, low, ORDERS - 1 - low)
    twice = 2 * np.arange(QUARTER)[:, None] + 1
    heads, tails = [], []
    for order in (even, ORDERS - 1 - even):
        weight = np.where(order == 0, 1.0, 2.0)
        angle = (order[None, :] * twice % (2 * NLON)) * (math.pi / NLON)
        for wave in (weight * np.cos(angle), -weight * np.sin(angle)):
            head = wave.astype(ml_dtypes.bfloat16)
            heads.append(head)
            tails.append((wave - head.astype(np.float64)).astype(ml_dtypes.bfloat16))
    return np.stack(heads + tails)


def nn(a, b):
    return lax.dot_general(a, b, (((1,), (0,)), ((), ())), preferred_element_type=F32)


def nt(a, b):
    return lax.dot_general(a, b, (((1,), (1,)), ((), ())), preferred_element_type=F32)


def kernel(
    state_hbm, table_hbm, low_hbm, lows_hbm, diffusion_hbm, coupling_hbm, waves, out,
    state, table, rows, low_row, lows, diffusion, coupling,
    wave_raw, wave_own, masked, st, cg, flat, s1, s2, r1, r2, s3, r3, mid, mid4, inv, send_x, recv_x, total,
    relay, load_sem, sem_cs, sem_cr, sem_1s, sem_1r, sem_2s, sem_2r, sem_3s, sem_3r, sem_us, sem_ur,
):
    slab = lax.axis_index("radial")
    mode = lax.axis_index("mode")
    far = mode // NEAR
    near = lax.rem(mode, NEAR)

    def x_peer(step):
        return lax.rem(slab + step, SLABS)

    def near_peer(step):
        return lax.rem(near // 2 + step[0], 4) * 2 + lax.rem(lax.rem(near, 2) + step[1], 2)

    def far_peer(step):
        return lax.rem(far + step, FAR)

    barrier = pltpu.get_barrier_semaphore()
    for step in X_STEPS:
        pl.semaphore_signal(barrier, inc=1, device_id=(x_peer(step), mode), device_id_type=MESH)
    for step in GREETED:
        pl.semaphore_signal(barrier, inc=1, device_id=(slab, far_peer(step) * NEAR + near), device_id_type=MESH)
    for step in NEAR_STEPS:
        pl.semaphore_signal(barrier, inc=1, device_id=(slab, far * NEAR + near_peer(step)), device_id_type=MESH)

    loads = [
        pltpu.make_async_copy(source, target, load_sem.at[i])
        for i, (source, target) in enumerate(
            (
                (lows_hbm, lows), (diffusion_hbm, diffusion), (coupling_hbm, coupling), (state_hbm, state),
                (table_hbm, table), (low_hbm, low_row), (waves, wave_raw),
            )
        )
    ]
    for load in loads:
        load.start()

    st[...] = jnp.zeros_like(st)
    mid4[...] = jnp.zeros_like(mid4)
    for load in loads[:4]:
        load.wait()
    for f in range(3):
        for s in range(2):
            for c in range(2):
                for p in range(2):
                    row = f * 8 + s * 4 + c * 2 + p
                    st[row : row + 1, 0:ROWS] = state[p, f, s, c : c + 1, :]
    cg[slab] = st[...].astype(BF16)

    def x_copy(source, target, i, send, recv):
        return pltpu.make_async_remote_copy(
            src_ref=source, dst_ref=target, send_sem=send.at[i], recv_sem=recv.at[i],
            device_id=(x_peer(X_STEPS[i]), mode), device_id_type=MESH,
        )

    def near_copies(source, target, send, recv):
        return [
            pltpu.make_async_remote_copy(
                src_ref=source.at[near_peer(step)], dst_ref=target.at[near], send_sem=send.at[i], recv_sem=recv.at[i],
                device_id=(slab, far * NEAR + near_peer(step)), device_id_type=MESH,
            )
            for i, step in enumerate(NEAR_STEPS)
        ]

    def far_copies(source, target, send, recv):
        return [
            pltpu.make_async_remote_copy(
                src_ref=source.at[far_peer(step)], dst_ref=target.at[far], send_sem=send.at[i], recv_sem=recv.at[i],
                device_id=(slab, far_peer(step) * NEAR + near), device_id_type=MESH,
            )
            for i, step in enumerate(FAR_STEPS)
        ]

    loads[4].wait()
    rows[...] = table[...].astype(F32).reshape(2 * ROWS, 128)
    for p in range(2):
        low = lows[mode * 2 + p]
        low_even = lax.rem(low, 2) == 0
        for start, size in ((0, 512), (512, 128)):
            row = lax.broadcasted_iota(jnp.int32, (size, 128), 0) + start
            if start == 0:
                values = rows[pl.ds(p, 512, stride=2), :]
            else:
                last = rows[1024 + p : 1025 + p, :]
                values = jnp.where(row == 512, jnp.broadcast_to(last, (128, 128)), 0.0)
            in_lower = row < ORDERS - low
            even_order = in_lower == low_even
            odd_sum = jnp.where(in_lower, lax.rem(row, 2), lax.rem(row + low, 2))
            sign = 1.0 - 2.0 * odd_sum.astype(F32)
            for q in range(2):
                north = jnp.where(even_order == (q == 0), values, 0.0)
                masked[p, start : start + size, q * 128 : (q + 1) * 128] = north.astype(BF16)
                masked[p, start : start + size, (2 + q) * 128 : (3 + q) * 128] = (north * sign).astype(BF16)

    pl.semaphore_wait(barrier, SLABS - 1 + NEAR - 1 + len(GREETED))

    coefs = [x_copy(cg.at[slab], cg.at[slab], i, sem_cs, sem_cr) for i in range(SLABS - 1)]
    for copy in coefs:
        copy.start()

    def pass_on(i, reach):
        for step in (reach, FAR - reach):
            pl.semaphore_signal(relay.at[i], inc=1, device_id=(slab, far_peer(step) * NEAR + near), device_id_type=MESH)

    pass_on(0, 2)

    pl.semaphore_wait(relay.at[0], 2)
    pass_on(1, 4)

    for copy in coefs:
        copy.wait()

    gathered = [cg[i].astype(F32) for i in range(SLABS)]
    lhs = jnp.concatenate(
        [gathered[i][f * 8 : (f + 1) * 8] for f in range(3) for i in range(SLABS)], axis=0
    ).astype(BF16)
    first_pair = lax.rem(lax.broadcasted_iota(jnp.int32, (96, 512), 0), 2) == 0
    synth = jnp.where(first_pair, nn(lhs, masked[0]), nn(lhs, masked[1]))
    for b in range(4):
        flat[b * 96 : (b + 1) * 96, :] = synth[:, b * 128 : (b + 1) * 128]
    for g in range(3):
        block = flat[g * 128 : (g + 1) * 128, :].T
        s1[:, :, g * 128 : (g + 1) * 128] = block.reshape(NEAR, FAR, 128).astype(BF16)
    hop1 = near_copies(s1, r1, sem_1s, sem_1r)
    for copy in hop1:
        copy.start()
    r1[near] = s1[near]

    for copy in hop1:
        copy.wait()
    arrived = r1[...].reshape(128, QUARTER).astype(F32)
    for g in range(3):
        mid[g] = arrived[:, g * 128 : (g + 1) * 128]
    for z in range(FAR):
        s2[z] = jnp.concatenate([mid[g, pl.ds(z, NEAR, stride=FAR), :] for g in range(3)], axis=0).astype(BF16)
    pl.semaphore_wait(relay.at[1], 2)
    hop2 = far_copies(s2, r2, sem_2s, sem_2r)
    for copy in hop2:
        copy.start()
    r2[far] = s2[far]

    for load in loads[5:]:
        load.wait()
    down = lax.broadcasted_iota(jnp.int32, (HALF, HALF), 0)
    across = lax.broadcasted_iota(jnp.int32, (HALF, HALF), 1)
    regroup = (down == lax.rem(across, 128) * 2 + across // 128).astype(F32).astype(BF16)
    natural = jnp.broadcast_to(low_row[...], (HALF, HALF))
    pick = nn((down == natural).astype(F32).astype(BF16), regroup).astype(BF16)
    lowest = pick[0:1, :].astype(F32)
    for q in range(8):
        wave_own[q] = nn(wave_raw[q], pick).astype(BF16)


    for copy in hop2:
        copy.wait()
    arrived = r2[...].astype(F32)
    for g in range(3):
        flat[g * 128 : (g + 1) * 128, :] = arrived[:, g * 8 : (g + 1) * 8, :].reshape(128, 128).T

    parts = []
    for q in range(2):
        for c in range(2):
            rows = [
                jnp.concatenate(
                    [flat[pl.ds((h * 2 + q) * 96 + c * 2 + p, 24, stride=4), :] for p in range(2)], axis=1
                )
                for h in range(2)
            ]
            data = jnp.concatenate(rows, axis=0).astype(BF16)
            at = q * 2 + c
            parts.append(nt(data, wave_own[at]) + nt(data, wave_own[4 + at]))
    a, b = parts[0] + parts[2], parts[1] + parts[3]
    c, d = parts[0] - parts[2], parts[1] - parts[3]
    images = (a + b, a - b, c - d, c + d)
    sums = [[], [], [], []]
    for h in range(2):
        for left, right in ((0, 1), (0, 2), (1, 2)):
            u, v = h * 24 + left * 8, h * 24 + right * 8
            p1, p2, p3, p4 = [image[u : u + 8] * image[v : v + 8] for image in images]
            both, across = p1 + p2, p3 + p4
            turn, twist = p1 - p2, p4 - p3
            sums[0].append(both + across)
            sums[1].append(turn + twist)
            sums[2].append(both - across)
            sums[3].append(turn - twist)
    for q in range(2):
        for c in range(2):
            at = q * 2 + c
            value = jnp.concatenate(sums[at], axis=0)
            head = value.astype(BF16)
            tail = (value - head.astype(F32)).astype(BF16)
            answer = nn(head, wave_own[at]) + (nn(tail, wave_own[at]) + nn(head, wave_own[4 + at]))
            if q == 0:
                answer = answer * (0.5 * KAPPA * (1.0 + lowest))
            else:
                answer = answer * (0.5 * KAPPA)
            for h in range(2):
                for p in range(2):
                    flat[pl.ds((h * 2 + q) * 96 + c * 2 + p, 24, stride=4), :] = answer[
                        h * 24 : (h + 1) * 24, p * 128 : (p + 1) * 128
                    ]
    for g in range(3):
        mid4[pl.ds(g, 128, stride=4), :] = flat[g * 128 : (g + 1) * 128, :].T
    s3[...] = mid4[...].reshape(128, 4, 128).astype(BF16)
    for z, y, c in ALL_STEPS:
        peer = far_peer(z) * NEAR + near_peer((y, c))
        pltpu.make_async_remote_copy(
            src_ref=s3.at[peer], dst_ref=r3.at[mode], send_sem=sem_3s.at[0], recv_sem=sem_3r.at[0],
            device_id=(slab, peer), device_id_type=MESH,
        ).start()
    r3[mode] = s3[mode]

    row8 = lax.broadcasted_iota(jnp.int32, (8, PADDED), 0)
    lane8 = lax.broadcasted_iota(jnp.int32, (8, PADDED), 1)
    low8 = jnp.where(lax.rem(row8, 2) == 0, lows[mode * 2], lows[mode * 2 + 1])
    degree = jnp.where(lane8 < ORDERS - low8, low8 + lane8, lane8 - 1).astype(F32)
    degree = degree * (degree + 1.0) * (shell_step * shell_step)
    first_shell = row8 < 4
    for f in range(3):
        diagonal = []
        for s in range(8):
            radius = inner_radius + (s + 0.5) * shell_step
            diagonal.append(degree * (1.0 / (radius * radius)) + (1.0 / diffusion[f] + 2.0))
        leading = [jnp.ones((8, PADDED), F32), diagonal[0]]
        trailing = [jnp.ones((8, PADDED), F32), diagonal[7]]
        for s in range(1, 8):
            leading.append(diagonal[s] * leading[s] - leading[s - 1])
            trailing.append(diagonal[7 - s] * trailing[s] - trailing[s - 1])
        share = 1.0 / leading[8]
        scaled = [value * share for value in leading]

        def entry(i, j):
            return scaled[min(i, j)] * trailing[7 - max(i, j)]

        for i in range(SLABS):
            for j in range(i, SLABS):
                inv[f, 0, i, j] = jnp.where(first_shell, entry(2 * i, 2 * j), entry(2 * i + 1, 2 * j + 1))
                inv[f, 1, i, j] = jnp.where(first_shell, entry(2 * i, 2 * j + 1), entry(2 * i + 1, 2 * j))
                if i != j:
                    inv[f, 0, j, i] = jnp.where(first_shell, entry(2 * i, 2 * j), entry(2 * i + 1, 2 * j + 1))
                    inv[f, 1, j, i] = jnp.where(first_shell, entry(2 * i + 1, 2 * j), entry(2 * i, 2 * j + 1))

    others = len(ALL_STEPS)
    pltpu.make_async_copy(r3.at[0:others], r3.at[0:others], sem_3r.at[0]).wait()
    pltpu.make_async_copy(s3.at[0:others], s3.at[0:others], sem_3s.at[0]).wait()

    mid4[...] = r3[...].astype(F32).reshape(512, 128)
    for g in range(3):
        flat[g * 128 : (g + 1) * 128, :] = jnp.concatenate(
            [mid4[pl.ds(y * 4 + g, FAR, stride=32), :] for y in range(NEAR)], axis=0
        ).T
    lhs = jnp.concatenate([flat[b * 96 : (b + 1) * 96, :] for b in range(4)], axis=1).astype(BF16)
    first_pair = lax.rem(lax.broadcasted_iota(jnp.int32, (96, PADDED), 0), 2) == 0
    nonlinear = jnp.where(first_pair, nt(lhs, masked[0]), nt(lhs, masked[1]))
    tails = [[] for _ in range(SLABS)]
    for f in range(3):
        own = st[f * 8 : (f + 1) * 8, :] * (2.0 / diffusion[f])
        drives, swapped = [], []
        for i in range(SLABS):
            start = f * 32 + i * 8
            mine = (slab == i).astype(F32)
            drive = nonlinear[start : start + 8] * coupling[f] + own * mine
            drives.append(drive)
            swapped.append(pltpu.roll(drive, 4, 0))
        for i in range(SLABS):
            value = inv[f, 0, i, 0] * drives[0] + inv[f, 1, i, 0] * swapped[0]
            for j in range(1, SLABS):
                value = value + inv[f, 0, i, j] * drives[j] + inv[f, 1, i, j] * swapped[j]
            for t in range(4):
                send_x[i, (f * 4 + t) * 8 : (f * 4 + t + 1) * 8, :] = value[:, t * 128 : (t + 1) * 128]
            tails[i].append(value[:, 512:PADDED])
    lane = lax.broadcasted_iota(jnp.int32, (8, 128), 1)
    for i in range(SLABS):
        send_x[i, 96:104, :] = jnp.where(
            lane == 0, tails[i][0], jnp.where(lane == 1, pltpu.roll(tails[i][1], 1, 1), pltpu.roll(tails[i][2], 2, 1))
        )
    last = [x_copy(send_x.at[x_peer(X_STEPS[i])], recv_x.at[i], i, sem_us, sem_ur) for i in range(SLABS - 1)]
    for copy in last:
        copy.start()
    for copy in last:
        copy.wait()
    whole = send_x[slab] + recv_x[0] + recv_x[1] + recv_x[2]
    for f in range(3):
        for t in range(4):
            tile = whole[(f * 4 + t) * 8 : (f * 4 + t + 1) * 8]
            total[f * 8 : (f + 1) * 8, t * 128 : (t + 1) * 128] = tile - st[f * 8 : (f + 1) * 8, t * 128 : (t + 1) * 128]
        total[f * 8 : (f + 1) * 8, 512:513] = whole[96:104, f : f + 1] - st[f * 8 : (f + 1) * 8, 512:513]
    for f in range(3):
        for s in range(2):
            for c in range(2):
                for p in range(2):
                    row = f * 8 + s * 4 + c * 2 + p
                    out[p, f, s, c : c + 1, :] = total[row : row + 1, 0:ROWS]


def body(spectral_state, synthesis_table, low_orders, diffusion, coupling):
    low_row = low_orders.reshape(1, HALF)
    vmem = pl.BlockSpec(memory_space=pltpu.VMEM)
    hbm = pl.BlockSpec(memory_space=pltpu.HBM)
    dma = pltpu.SemaphoreType.DMA
    return pl.pallas_call(
        kernel,
        out_shape=pltpu.VMEM(spectral_state.shape, F32),
        in_specs=[hbm] * 7,
        out_specs=vmem,
        scratch_shapes=[
            pltpu.VMEM(spectral_state.shape, F32),
            pltpu.VMEM((ROWS, 2, 128), BF16),
            pltpu.VMEM((2 * ROWS, 128), F32),
            pltpu.VMEM((1, HALF), jnp.int32),
            pltpu.SMEM((HALF,), jnp.int32),
            pltpu.SMEM((3,), F32),
            pltpu.SMEM((3,), F32),
            pltpu.VMEM((8, QUARTER, HALF), BF16),
            pltpu.VMEM((8, QUARTER, HALF), BF16),
            pltpu.VMEM((2, PADDED, 512), BF16),
            pltpu.VMEM((24, PADDED), F32),
            pltpu.VMEM((SLABS, 24, PADDED), BF16),
            pltpu.VMEM((384, 128), F32),
            pltpu.VMEM((NEAR, FAR, 384), BF16),
            pltpu.VMEM((FAR, 24, 128), BF16),
            pltpu.VMEM((NEAR, FAR, 384), BF16),
            pltpu.VMEM((FAR, 24, 128), BF16),
            pltpu.VMEM((128, 4, 128), BF16),
            pltpu.VMEM((128, 4, 128), BF16),
            pltpu.VMEM((3, 128, 128), F32),
            pltpu.VMEM((512, 128), F32),
            pltpu.VMEM((3, 2, SLABS, SLABS, 8, PADDED), F32),
            pltpu.VMEM((SLABS, 104, 128), F32),
            pltpu.VMEM((SLABS - 1, 104, 128), F32),
            pltpu.VMEM((24, PADDED), F32),
            pltpu.SemaphoreType.REGULAR((2,)),
            dma((7,)),
            dma((SLABS - 1,)), dma((SLABS - 1,)),
            dma((NEAR - 1,)), dma((NEAR - 1,)),
            dma((FAR - 1,)), dma((FAR - 1,)),
            dma((1,)), dma((1,)),
            dma((SLABS - 1,)), dma((SLABS - 1,)),
        ],
        compiler_params=pltpu.CompilerParams(
            collective_id=0, has_side_effects=True, vmem_limit_bytes=63 * 1024 * 1024
        ),
    )(spectral_state, jnp.transpose(synthesis_table, (1, 0, 2)), low_row, low_orders, diffusion, coupling, jnp.asarray(wave_tables()))


def solution(mesh):
    placed = (P("mode", None, "radial", None, None), P("mode", None, "radial"), P(), P(), P())
    return jax.shard_map(
        body,
        mesh=mesh,
        in_specs=placed,
        out_specs=P("mode", None, "radial", None, None),
        check_vma=False,
    )
```

```python
import math

import jax
import jax.numpy as jnp
import ml_dtypes
import numpy as np
from jax import lax
from jax.experimental import pallas as pl
from jax.experimental.pallas import tpu as pltpu
from jax.sharding import PartitionSpec as P

inner_radius = 0.538
shell_step = 1.0 / 2048.0

ORDERS = 512
HALF = 256
ROWS = 513
PADDED = 640
NLON = 1536
QUARTER = 384
NLAT = 1024
SLABS = 4
NEAR = 8
FAR = 16
X_STEPS = (2, 1, 3)
NEAR_STEPS = ((2, 0), (2, 1), (1, 0), (3, 0), (1, 1), (3, 1), (0, 1))
FAR_STEPS = (8, 7, 9, 6, 10, 5, 11, 4, 12, 3, 13, 2, 14, 1, 15)
ALL_STEPS = sorted(
    ((z, y, c) for z in range(FAR) for y in range(4) for c in range(2) if z or y or c),
    key=lambda step: (-min(step[0], FAR - step[0]) - min(step[1], 4 - step[1]), step),
)
GREETED = (2, 14, 1, 15)
KAPPA = 2.0 * math.sqrt(ORDERS * (ORDERS + 1) / (NLAT * NLON))
MESH = pl.DeviceIdType.MESH
F32 = jnp.float32
BF16 = jnp.bfloat16


def wave_tables():
    low = np.arange(HALF)
    even = np.where(low % 2 == 0, low, ORDERS - 1 - low)
    twice = 2 * np.arange(QUARTER)[:, None] + 1
    heads, tails = [], []
    for order in (even, ORDERS - 1 - even):
        weight = np.where(order == 0, 1.0, 2.0)
        angle = (order[None, :] * twice % (2 * NLON)) * (math.pi / NLON)
        for wave in (weight * np.cos(angle), -weight * np.sin(angle)):
            head = wave.astype(ml_dtypes.bfloat16)
            heads.append(head)
            tails.append((wave - head.astype(np.float64)).astype(ml_dtypes.bfloat16))
    return np.stack(heads + tails)


def nn(a, b):
    return lax.dot_general(a, b, (((1,), (0,)), ((), ())), preferred_element_type=F32)


def nt(a, b):
    return lax.dot_general(a, b, (((1,), (1,)), ((), ())), preferred_element_type=F32)


def kernel(
    state_hbm, table_hbm, low_hbm, lows_hbm, diffusion_hbm, coupling_hbm, waves, out,
    state, table, rows, low_row, lows, diffusion, coupling,
    wave_raw, wave_own, masked, st, cg, flat, s1, s2, r1, r2, s3, r3, mid, mid4, inv, send_x, recv_x, total,
    relay, load_sem, sem_cs, sem_cr, sem_1s, sem_1r, sem_2s, sem_2r, sem_3s, sem_3r, sem_us, sem_ur,
):
    slab = lax.axis_index("radial")
    mode = lax.axis_index("mode")
    far = mode // NEAR
    near = lax.rem(mode, NEAR)

    def x_peer(step):
        return lax.rem(slab + step, SLABS)

    def near_peer(step):
        return lax.rem(near // 2 + step[0], 4) * 2 + lax.rem(lax.rem(near, 2) + step[1], 2)

    def far_peer(step):
        return lax.rem(far + step, FAR)

    barrier = pltpu.get_barrier_semaphore()
    for step in GREETED:
        pl.semaphore_signal(barrier, inc=1, device_id=(slab, far_peer(step) * NEAR + near), device_id_type=MESH)
    for step in NEAR_STEPS:
        pl.semaphore_signal(barrier, inc=1, device_id=(slab, far * NEAR + near_peer(step)), device_id_type=MESH)
    for step in X_STEPS:
        pl.semaphore_signal(barrier, inc=1, device_id=(x_peer(step), mode), device_id_type=MESH)

    loads = [
        pltpu.make_async_copy(source, target, load_sem.at[i])
        for i, (source, target) in enumerate(
            (
                (lows_hbm, lows), (diffusion_hbm, diffusion), (coupling_hbm, coupling), (state_hbm, state),
                (table_hbm, table), (low_hbm, low_row), (waves, wave_raw),
            )
        )
    ]
    for load in loads:
        load.start()

    st[...] = jnp.zeros_like(st)
    mid4[...] = jnp.zeros_like(mid4)
    for load in loads[:4]:
        load.wait()
    for f in range(3):
        for s in range(2):
            for c in range(2):
                for p in range(2):
                    row = f * 8 + s * 4 + c * 2 + p
                    st[row : row + 1, 0:ROWS] = state[p, f, s, c : c + 1, :]
    cg[slab] = st[...].astype(BF16)

    def x_copy(source, target, i, send, recv):
        return pltpu.make_async_remote_copy(
            src_ref=source, dst_ref=target, send_sem=send.at[i], recv_sem=recv.at[i],
            device_id=(x_peer(X_STEPS[i]), mode), device_id_type=MESH,
        )

    def near_copies(source, target, send, recv):
        return [
            pltpu.make_async_remote_copy(
                src_ref=source.at[near_peer(step)], dst_ref=target.at[near], send_sem=send.at[i], recv_sem=recv.at[i],
                device_id=(slab, far * NEAR + near_peer(step)), device_id_type=MESH,
            )
            for i, step in enumerate(NEAR_STEPS)
        ]

    def far_copies(source, target, send, recv):
        return [
            pltpu.make_async_remote_copy(
                src_ref=source.at[far_peer(step)], dst_ref=target.at[far], send_sem=send.at[i], recv_sem=recv.at[i],
                device_id=(slab, far_peer(step) * NEAR + near), device_id_type=MESH,
            )
            for i, step in enumerate(FAR_STEPS)
        ]

    loads[4].wait()
    rows[...] = table[...].astype(F32).reshape(2 * ROWS, 128)
    for p in range(2):
        low = lows[mode * 2 + p]
        low_even = lax.rem(low, 2) == 0
        for start, size in ((0, 512), (512, 128)):
            row = lax.broadcasted_iota(jnp.int32, (size, 128), 0) + start
            if start == 0:
                values = rows[pl.ds(p, 512, stride=2), :]
            else:
                last = rows[1024 + p : 1025 + p, :]
                values = jnp.where(row == 512, jnp.broadcast_to(last, (128, 128)), 0.0)
            in_lower = row < ORDERS - low
            even_order = in_lower == low_even
            odd_sum = jnp.where(in_lower, lax.rem(row, 2), lax.rem(row + low, 2))
            sign = 1.0 - 2.0 * odd_sum.astype(F32)
            for q in range(2):
                north = jnp.where(even_order == (q == 0), values, 0.0)
                masked[p, start : start + size, q * 128 : (q + 1) * 128] = north.astype(BF16)
                masked[p, start : start + size, (2 + q) * 128 : (3 + q) * 128] = (north * sign).astype(BF16)

    pl.semaphore_wait(barrier, SLABS - 1 + NEAR - 1 + len(GREETED))

    coefs = [x_copy(cg.at[slab], cg.at[slab], i, sem_cs, sem_cr) for i in range(SLABS - 1)]
    for copy in coefs:
        copy.start()

    def pass_on(i, reach):
        for step in (reach, FAR - reach):
            pl.semaphore_signal(relay.at[i], inc=1, device_id=(slab, far_peer(step) * NEAR + near), device_id_type=MESH)

    pass_on(0, 2)

    pl.semaphore_wait(relay.at[0], 2)
    pass_on(1, 4)

    for copy in coefs:
        copy.wait()

    gathered = [cg[i].astype(F32) for i in range(SLABS)]
    lhs = jnp.concatenate(
        [gathered[i][f * 8 : (f + 1) * 8] for f in range(3) for i in range(SLABS)], axis=0
    ).astype(BF16)
    first_pair = lax.rem(lax.broadcasted_iota(jnp.int32, (96, 512), 0), 2) == 0
    synth = jnp.where(first_pair, nn(lhs, masked[0]), nn(lhs, masked[1]))
    for b in range(4):
        flat[b * 96 : (b + 1) * 96, :] = synth[:, b * 128 : (b + 1) * 128]
    for g in range(3):
        block = flat[g * 128 : (g + 1) * 128, :].T
        s1[:, :, g * 128 : (g + 1) * 128] = block.reshape(NEAR, FAR, 128).astype(BF16)
    hop1 = near_copies(s1, r1, sem_1s, sem_1r)
    for copy in hop1:
        copy.start()
    r1[near] = s1[near]

    for copy in hop1:
        copy.wait()
    arrived = r1[...].reshape(128, QUARTER).astype(F32)
    for g in range(3):
        mid[g] = arrived[:, g * 128 : (g + 1) * 128]
    for z in range(FAR):
        s2[z] = jnp.concatenate([mid[g, pl.ds(z, NEAR, stride=FAR), :] for g in range(3)], axis=0).astype(BF16)
    pl.semaphore_wait(relay.at[1], 2)
    hop2 = far_copies(s2, r2, sem_2s, sem_2r)
    for copy in hop2:
        copy.start()
    r2[far] = s2[far]

    for load in loads[5:]:
        load.wait()
    down = lax.broadcasted_iota(jnp.int32, (HALF, HALF), 0)
    across = lax.broadcasted_iota(jnp.int32, (HALF, HALF), 1)
    regroup = (down == lax.rem(across, 128) * 2 + across // 128).astype(F32).astype(BF16)
    natural = jnp.broadcast_to(low_row[...], (HALF, HALF))
    pick = nn((down == natural).astype(F32).astype(BF16), regroup).astype(BF16)
    lowest = pick[0:1, :].astype(F32)
    for q in range(8):
        wave_own[q] = nn(wave_raw[q], pick).astype(BF16)


    for copy in hop2:
        copy.wait()
    arrived = r2[...].astype(F32)
    for g in range(3):
        flat[g * 128 : (g + 1) * 128, :] = arrived[:, g * 8 : (g + 1) * 8, :].reshape(128, 128).T

    parts = []
    for q in range(2):
        for c in range(2):
            rows = [
                jnp.concatenate(
                    [flat[pl.ds((h * 2 + q) * 96 + c * 2 + p, 24, stride=4), :] for p in range(2)], axis=1
                )
                for h in range(2)
            ]
            data = jnp.concatenate(rows, axis=0).astype(BF16)
            at = q * 2 + c
            parts.append(nt(data, wave_own[at]) + nt(data, wave_own[4 + at]))
    a, b = parts[0] + parts[2], parts[1] + parts[3]
    c, d = parts[0] - parts[2], parts[1] - parts[3]
    images = (a + b, a - b, c - d, c + d)
    sums = [[], [], [], []]
    for h in range(2):
        for left, right in ((0, 1), (0, 2), (1, 2)):
            u, v = h * 24 + left * 8, h * 24 + right * 8
            p1, p2, p3, p4 = [image[u : u + 8] * image[v : v + 8] for image in images]
            both, across = p1 + p2, p3 + p4
            turn, twist = p1 - p2, p4 - p3
            sums[0].append(both + across)
            sums[1].append(turn + twist)
            sums[2].append(both - across)
            sums[3].append(turn - twist)
    for q in range(2):
        for c in range(2):
            at = q * 2 + c
            value = jnp.concatenate(sums[at], axis=0)
            head = value.astype(BF16)
            tail = (value - head.astype(F32)).astype(BF16)
            answer = nn(head, wave_own[at]) + (nn(tail, wave_own[at]) + nn(head, wave_own[4 + at]))
            if q == 0:
                answer = answer * (0.5 * KAPPA * (1.0 + lowest))
            else:
                answer = answer * (0.5 * KAPPA)
            for h in range(2):
                for p in range(2):
                    flat[pl.ds((h * 2 + q) * 96 + c * 2 + p, 24, stride=4), :] = answer[
                        h * 24 : (h + 1) * 24, p * 128 : (p + 1) * 128
                    ]
    for g in range(3):
        mid4[pl.ds(g, 128, stride=4), :] = flat[g * 128 : (g + 1) * 128, :].T
    s3[...] = mid4[...].reshape(128, 4, 128).astype(BF16)
    for z, y, c in ALL_STEPS:
        peer = far_peer(z) * NEAR + near_peer((y, c))
        pltpu.make_async_remote_copy(
            src_ref=s3.at[peer], dst_ref=r3.at[mode], send_sem=sem_3s.at[0], recv_sem=sem_3r.at[0],
            device_id=(slab, peer), device_id_type=MESH,
        ).start()
    r3[mode] = s3[mode]

    row8 = lax.broadcasted_iota(jnp.int32, (8, PADDED), 0)
    lane8 = lax.broadcasted_iota(jnp.int32, (8, PADDED), 1)
    low8 = jnp.where(lax.rem(row8, 2) == 0, lows[mode * 2], lows[mode * 2 + 1])
    degree = jnp.where(lane8 < ORDERS - low8, low8 + lane8, lane8 - 1).astype(F32)
    degree = degree * (degree + 1.0) * (shell_step * shell_step)
    first_shell = row8 < 4
    for f in range(3):
        diagonal = []
        for s in range(8):
            radius = inner_radius + (s + 0.5) * shell_step
            diagonal.append(degree * (1.0 / (radius * radius)) + (1.0 / diffusion[f] + 2.0))
        leading = [jnp.ones((8, PADDED), F32), diagonal[0]]
        trailing = [jnp.ones((8, PADDED), F32), diagonal[7]]
        for s in range(1, 8):
            leading.append(diagonal[s] * leading[s] - leading[s - 1])
            trailing.append(diagonal[7 - s] * trailing[s] - trailing[s - 1])
        share = 1.0 / leading[8]
        scaled = [value * share for value in leading]

        def entry(i, j):
            return scaled[min(i, j)] * trailing[7 - max(i, j)]

        for i in range(SLABS):
            for j in range(i, SLABS):
                inv[f, 0, i, j] = jnp.where(first_shell, entry(2 * i, 2 * j), entry(2 * i + 1, 2 * j + 1))
                inv[f, 1, i, j] = jnp.where(first_shell, entry(2 * i, 2 * j + 1), entry(2 * i + 1, 2 * j))
                if i != j:
                    inv[f, 0, j, i] = jnp.where(first_shell, entry(2 * i, 2 * j), entry(2 * i + 1, 2 * j + 1))
                    inv[f, 1, j, i] = jnp.where(first_shell, entry(2 * i + 1, 2 * j), entry(2 * i, 2 * j + 1))

    others = len(ALL_STEPS)
    pltpu.make_async_copy(r3.at[0:others], r3.at[0:others], sem_3r.at[0]).wait()
    pltpu.make_async_copy(s3.at[0:others], s3.at[0:others], sem_3s.at[0]).wait()

    mid4[...] = r3[...].astype(F32).reshape(512, 128)
    for g in range(3):
        flat[g * 128 : (g + 1) * 128, :] = jnp.concatenate(
            [mid4[pl.ds(y * 4 + g, FAR, stride=32), :] for y in range(NEAR)], axis=0
        ).T
    lhs = jnp.concatenate([flat[b * 96 : (b + 1) * 96, :] for b in range(4)], axis=1).astype(BF16)
    first_pair = lax.rem(lax.broadcasted_iota(jnp.int32, (96, PADDED), 0), 2) == 0
    nonlinear = jnp.where(first_pair, nt(lhs, masked[0]), nt(lhs, masked[1]))
    last = []
    for f in range(3):
        own = st[f * 8 : (f + 1) * 8, :] * (2.0 / diffusion[f])
        drives, swapped = [], []
        for i in range(SLABS):
            start = f * 32 + i * 8
            mine = (slab == i).astype(F32)
            drive = nonlinear[start : start + 8] * coupling[f] + own * mine
            drives.append(drive)
            swapped.append(pltpu.roll(drive, 4, 0))
        for i in range(SLABS):
            value = inv[f, 0, i, 0] * drives[0] + inv[f, 1, i, 0] * swapped[0]
            for j in range(1, SLABS):
                value = value + inv[f, 0, i, j] * drives[j] + inv[f, 1, i, j] * swapped[j]
            send_x[i, f] = value
        for i in range(SLABS - 1):
            last.append(
                pltpu.make_async_remote_copy(
                    src_ref=send_x.at[x_peer(X_STEPS[i]), f], dst_ref=recv_x.at[i, f],
                    send_sem=sem_us.at[f * 3 + i], recv_sem=sem_ur.at[f * 3 + i],
                    device_id=(x_peer(X_STEPS[i]), mode), device_id_type=MESH,
                )
            )
            last[-1].start()
    total[...] = send_x[slab].reshape(24, PADDED) - st[...]
    for copy in last:
        copy.wait()
    total[...] = total[...] + (recv_x[0] + recv_x[1] + recv_x[2]).reshape(24, PADDED)
    for f in range(3):
        for s in range(2):
            for c in range(2):
                for p in range(2):
                    row = f * 8 + s * 4 + c * 2 + p
                    out[p, f, s, c : c + 1, :] = total[row : row + 1, 0:ROWS]


def body(spectral_state, synthesis_table, low_orders, diffusion, coupling):
    low_row = low_orders.reshape(1, HALF)
    vmem = pl.BlockSpec(memory_space=pltpu.VMEM)
    hbm = pl.BlockSpec(memory_space=pltpu.HBM)
    dma = pltpu.SemaphoreType.DMA
    return pl.pallas_call(
        kernel,
        out_shape=pltpu.VMEM(spectral_state.shape, F32),
        in_specs=[hbm] * 7,
        out_specs=vmem,
        scratch_shapes=[
            pltpu.VMEM(spectral_state.shape, F32),
            pltpu.VMEM((ROWS, 2, 128), BF16),
            pltpu.VMEM((2 * ROWS, 128), F32),
            pltpu.VMEM((1, HALF), jnp.int32),
            pltpu.SMEM((HALF,), jnp.int32),
            pltpu.SMEM((3,), F32),
            pltpu.SMEM((3,), F32),
            pltpu.VMEM((8, QUARTER, HALF), BF16),
            pltpu.VMEM((8, QUARTER, HALF), BF16),
            pltpu.VMEM((2, PADDED, 512), BF16),
            pltpu.VMEM((24, PADDED), F32),
            pltpu.VMEM((SLABS, 24, PADDED), BF16),
            pltpu.VMEM((384, 128), F32),
            pltpu.VMEM((NEAR, FAR, 384), BF16),
            pltpu.VMEM((FAR, 24, 128), BF16),
            pltpu.VMEM((NEAR, FAR, 384), BF16),
            pltpu.VMEM((FAR, 24, 128), BF16),
            pltpu.VMEM((128, 4, 128), BF16),
            pltpu.VMEM((128, 4, 128), BF16),
            pltpu.VMEM((3, 128, 128), F32),
            pltpu.VMEM((512, 128), F32),
            pltpu.VMEM((3, 2, SLABS, SLABS, 8, PADDED), F32),
            pltpu.VMEM((SLABS, 3, 8, PADDED), F32),
            pltpu.VMEM((SLABS - 1, 3, 8, PADDED), F32),
            pltpu.VMEM((24, PADDED), F32),
            pltpu.SemaphoreType.REGULAR((2,)),
            dma((7,)),
            dma((SLABS - 1,)), dma((SLABS - 1,)),
            dma((NEAR - 1,)), dma((NEAR - 1,)),
            dma((FAR - 1,)), dma((FAR - 1,)),
            dma((1,)), dma((1,)),
            dma((9,)), dma((9,)),
        ],
        compiler_params=pltpu.CompilerParams(
            collective_id=0, has_side_effects=True, vmem_limit_bytes=63 * 1024 * 1024
        ),
    )(spectral_state, jnp.transpose(synthesis_table, (1, 0, 2)), low_row, low_orders, diffusion, coupling, jnp.asarray(wave_tables()))


def solution(mesh):
    placed = (P("mode", None, "radial", None, None), P("mode", None, "radial"), P(), P(), P())
    return jax.shard_map(
        body,
        mesh=mesh,
        in_specs=placed,
        out_specs=P("mode", None, "radial", None, None),
        check_vma=False,
    )
```

```python
import math

import jax
import jax.numpy as jnp
import ml_dtypes
import numpy as np
from jax import lax
from jax.experimental import pallas as pl
from jax.experimental.pallas import tpu as pltpu
from jax.sharding import PartitionSpec as P

inner_radius = 0.538
shell_step = 1.0 / 2048.0

ORDERS = 512
HALF = 256
ROWS = 513
PADDED = 640
NLON = 1536
QUARTER = 384
NLAT = 1024
SLABS = 4
NEAR = 8
FAR = 16
X_STEPS = (2, 1, 3)
NEAR_STEPS = ((2, 0), (2, 1), (1, 0), (3, 0), (1, 1), (3, 1), (0, 1))
FAR_STEPS = (8, 7, 9, 6, 10, 5, 11, 4, 12, 3, 13, 2, 14, 1, 15)
ALL_STEPS = sorted(
    ((z, y, c) for z in range(FAR) for y in range(4) for c in range(2) if z or y or c),
    key=lambda step: (-min(step[0], FAR - step[0]) - min(step[1], 4 - step[1]), step),
)
GREETED = (2, 14, 1, 15)
KAPPA = 2.0 * math.sqrt(ORDERS * (ORDERS + 1) / (NLAT * NLON))
MESH = pl.DeviceIdType.MESH
F32 = jnp.float32
BF16 = jnp.bfloat16


def wave_tables():
    low = np.arange(HALF)
    even = np.where(low % 2 == 0, low, ORDERS - 1 - low)
    twice = 2 * np.arange(QUARTER)[:, None] + 1
    heads, tails = [], []
    for order in (even, ORDERS - 1 - even):
        weight = np.where(order == 0, 1.0, 2.0)
        angle = (order[None, :] * twice % (2 * NLON)) * (math.pi / NLON)
        for wave in (weight * np.cos(angle), -weight * np.sin(angle)):
            head = wave.astype(ml_dtypes.bfloat16)
            heads.append(head)
            tails.append((wave - head.astype(np.float64)).astype(ml_dtypes.bfloat16))
    return np.stack(heads + tails)


def nn(a, b):
    return lax.dot_general(a, b, (((1,), (0,)), ((), ())), preferred_element_type=F32)


def nt(a, b):
    return lax.dot_general(a, b, (((1,), (1,)), ((), ())), preferred_element_type=F32)


def kernel(
    state_hbm, table_hbm, low_hbm, lows_hbm, diffusion_hbm, coupling_hbm, waves, out,
    state, table, rows, low_row, lows, diffusion, coupling,
    wave_raw, wave_own, masked, st, cg, flat, s1, s2, r1, r2, s3, r3, mid, mid4, inv, send_x, recv_x, total,
    relay, load_sem, sem_cs, sem_cr, sem_1s, sem_1r, sem_2s, sem_2r, sem_3s, sem_3r, sem_us, sem_ur,
):
    slab = lax.axis_index("radial")
    mode = lax.axis_index("mode")
    far = mode // NEAR
    near = lax.rem(mode, NEAR)

    def x_peer(step):
        return lax.rem(slab + step, SLABS)

    def near_peer(step):
        return lax.rem(near // 2 + step[0], 4) * 2 + lax.rem(lax.rem(near, 2) + step[1], 2)

    def far_peer(step):
        return lax.rem(far + step, FAR)

    barrier = pltpu.get_barrier_semaphore()
    for step in GREETED:
        pl.semaphore_signal(barrier, inc=1, device_id=(slab, far_peer(step) * NEAR + near), device_id_type=MESH)
    for step in NEAR_STEPS:
        pl.semaphore_signal(barrier, inc=1, device_id=(slab, far * NEAR + near_peer(step)), device_id_type=MESH)
    for step in X_STEPS:
        pl.semaphore_signal(barrier, inc=1, device_id=(x_peer(step), mode), device_id_type=MESH)

    loads = [
        pltpu.make_async_copy(source, target, load_sem.at[i])
        for i, (source, target) in enumerate(
            (
                (lows_hbm, lows), (diffusion_hbm, diffusion), (coupling_hbm, coupling), (state_hbm, state),
                (table_hbm, table), (low_hbm, low_row), (waves, wave_raw),
            )
        )
    ]
    for load in loads:
        load.start()

    st[...] = jnp.zeros_like(st)
    mid4[...] = jnp.zeros_like(mid4)
    for load in loads[:4]:
        load.wait()
    for f in range(3):
        for s in range(2):
            for c in range(2):
                for p in range(2):
                    row = f * 8 + s * 4 + c * 2 + p
                    st[row : row + 1, 0:ROWS] = state[p, f, s, c : c + 1, :]
    cg[slab] = st[...].astype(BF16)

    def x_copy(source, target, i, send, recv):
        return pltpu.make_async_remote_copy(
            src_ref=source, dst_ref=target, send_sem=send.at[i], recv_sem=recv.at[i],
            device_id=(x_peer(X_STEPS[i]), mode), device_id_type=MESH,
        )

    def near_copies(source, target, send, recv):
        return [
            pltpu.make_async_remote_copy(
                src_ref=source.at[near_peer(step)], dst_ref=target.at[near], send_sem=send.at[i], recv_sem=recv.at[i],
                device_id=(slab, far * NEAR + near_peer(step)), device_id_type=MESH,
            )
            for i, step in enumerate(NEAR_STEPS)
        ]

    def far_copies(source, target, send, recv):
        return [
            pltpu.make_async_remote_copy(
                src_ref=source.at[far_peer(step)], dst_ref=target.at[far], send_sem=send.at[i], recv_sem=recv.at[i],
                device_id=(slab, far_peer(step) * NEAR + near), device_id_type=MESH,
            )
            for i, step in enumerate(FAR_STEPS)
        ]

    loads[4].wait()
    rows[...] = table[...].astype(F32).reshape(2 * ROWS, 128)
    for p in range(2):
        low = lows[mode * 2 + p]
        low_even = lax.rem(low, 2) == 0
        for start, size in ((0, 512), (512, 128)):
            row = lax.broadcasted_iota(jnp.int32, (size, 128), 0) + start
            if start == 0:
                values = rows[pl.ds(p, 512, stride=2), :]
            else:
                last = rows[1024 + p : 1025 + p, :]
                values = jnp.where(row == 512, jnp.broadcast_to(last, (128, 128)), 0.0)
            in_lower = row < ORDERS - low
            even_order = in_lower == low_even
            odd_sum = jnp.where(in_lower, lax.rem(row, 2), lax.rem(row + low, 2))
            sign = 1.0 - 2.0 * odd_sum.astype(F32)
            for q in range(2):
                north = jnp.where(even_order == (q == 0), values, 0.0)
                masked[p, start : start + size, q * 128 : (q + 1) * 128] = north.astype(BF16)
                masked[p, start : start + size, (2 + q) * 128 : (3 + q) * 128] = (north * sign).astype(BF16)

    pl.semaphore_wait(barrier, SLABS - 1 + NEAR - 1 + len(GREETED))

    coefs = [x_copy(cg.at[slab], cg.at[slab], i, sem_cs, sem_cr) for i in range(SLABS - 1)]
    for copy in coefs:
        copy.start()

    def pass_on(i, reach):
        for step in (reach, FAR - reach):
            pl.semaphore_signal(relay.at[i], inc=1, device_id=(slab, far_peer(step) * NEAR + near), device_id_type=MESH)

    pass_on(0, 2)

    pl.semaphore_wait(relay.at[0], 2)
    pass_on(1, 4)

    for copy in coefs:
        copy.wait_recv()

    gathered = [cg[i].astype(F32) for i in range(SLABS)]
    lhs = jnp.concatenate(
        [gathered[i][f * 8 : (f + 1) * 8] for f in range(3) for i in range(SLABS)], axis=0
    ).astype(BF16)
    first_pair = lax.rem(lax.broadcasted_iota(jnp.int32, (96, 512), 0), 2) == 0
    synth = jnp.where(first_pair, nn(lhs, masked[0]), nn(lhs, masked[1]))
    for b in range(4):
        flat[b * 96 : (b + 1) * 96, :] = synth[:, b * 128 : (b + 1) * 128]
    for g in range(3):
        block = flat[g * 128 : (g + 1) * 128, :].T
        s1[:, :, g * 128 : (g + 1) * 128] = block.reshape(NEAR, FAR, 128).astype(BF16)
    hop1 = near_copies(s1, r1, sem_1s, sem_1r)
    for copy in hop1:
        copy.start()
    r1[near] = s1[near]

    for copy in hop1:
        copy.wait_recv()
    arrived = r1[...].reshape(128, QUARTER).astype(F32)
    for g in range(3):
        mid[g] = arrived[:, g * 128 : (g + 1) * 128]
    for z in range(FAR):
        s2[z] = jnp.concatenate([mid[g, pl.ds(z, NEAR, stride=FAR), :] for g in range(3)], axis=0).astype(BF16)
    pl.semaphore_wait(relay.at[1], 2)
    hop2 = far_copies(s2, r2, sem_2s, sem_2r)
    for copy in hop2:
        copy.start()
    r2[far] = s2[far]

    for load in loads[5:]:
        load.wait()
    down = lax.broadcasted_iota(jnp.int32, (HALF, HALF), 0)
    across = lax.broadcasted_iota(jnp.int32, (HALF, HALF), 1)
    regroup = (down == lax.rem(across, 128) * 2 + across // 128).astype(F32).astype(BF16)
    natural = jnp.broadcast_to(low_row[...], (HALF, HALF))
    pick = nn((down == natural).astype(F32).astype(BF16), regroup).astype(BF16)
    lowest = pick[0:1, :].astype(F32)
    for q in range(8):
        wave_own[q] = nn(wave_raw[q], pick).astype(BF16)


    for copy in hop2:
        copy.wait_recv()
    arrived = r2[...].astype(F32)
    for g in range(3):
        flat[g * 128 : (g + 1) * 128, :] = arrived[:, g * 8 : (g + 1) * 8, :].reshape(128, 128).T

    parts = []
    for q in range(2):
        for c in range(2):
            rows = [
                jnp.concatenate(
                    [flat[pl.ds((h * 2 + q) * 96 + c * 2 + p, 24, stride=4), :] for p in range(2)], axis=1
                )
                for h in range(2)
            ]
            data = jnp.concatenate(rows, axis=0).astype(BF16)
            at = q * 2 + c
            parts.append(nt(data, wave_own[at]) + nt(data, wave_own[4 + at]))
    a, b = parts[0] + parts[2], parts[1] + parts[3]
    c, d = parts[0] - parts[2], parts[1] - parts[3]
    images = (a + b, a - b, c - d, c + d)
    sums = [[], [], [], []]
    for h in range(2):
        for left, right in ((0, 1), (0, 2), (1, 2)):
            u, v = h * 24 + left * 8, h * 24 + right * 8
            p1, p2, p3, p4 = [image[u : u + 8] * image[v : v + 8] for image in images]
            both, across = p1 + p2, p3 + p4
            turn, twist = p1 - p2, p4 - p3
            sums[0].append(both + across)
            sums[1].append(turn + twist)
            sums[2].append(both - across)
            sums[3].append(turn - twist)
    for q in range(2):
        for c in range(2):
            at = q * 2 + c
            value = jnp.concatenate(sums[at], axis=0)
            head = value.astype(BF16)
            tail = (value - head.astype(F32)).astype(BF16)
            answer = nn(head, wave_own[at]) + (nn(tail, wave_own[at]) + nn(head, wave_own[4 + at]))
            if q == 0:
                answer = answer * (0.5 * KAPPA * (1.0 + lowest))
            else:
                answer = answer * (0.5 * KAPPA)
            for h in range(2):
                for p in range(2):
                    flat[pl.ds((h * 2 + q) * 96 + c * 2 + p, 24, stride=4), :] = answer[
                        h * 24 : (h + 1) * 24, p * 128 : (p + 1) * 128
                    ]
    for g in range(3):
        mid4[pl.ds(g, 128, stride=4), :] = flat[g * 128 : (g + 1) * 128, :].T
    s3[...] = mid4[...].reshape(128, 4, 128).astype(BF16)
    for z, y, c in ALL_STEPS:
        peer = far_peer(z) * NEAR + near_peer((y, c))
        pltpu.make_async_remote_copy(
            src_ref=s3.at[peer], dst_ref=r3.at[mode], send_sem=sem_3s.at[0], recv_sem=sem_3r.at[0],
            device_id=(slab, peer), device_id_type=MESH,
        ).start()
    r3[mode] = s3[mode]

    row8 = lax.broadcasted_iota(jnp.int32, (8, PADDED), 0)
    lane8 = lax.broadcasted_iota(jnp.int32, (8, PADDED), 1)
    low8 = jnp.where(lax.rem(row8, 2) == 0, lows[mode * 2], lows[mode * 2 + 1])
    degree = jnp.where(lane8 < ORDERS - low8, low8 + lane8, lane8 - 1).astype(F32)
    degree = degree * (degree + 1.0) * (shell_step * shell_step)
    first_shell = row8 < 4
    for f in range(3):
        diagonal = []
        for s in range(8):
            radius = inner_radius + (s + 0.5) * shell_step
            diagonal.append(degree * (1.0 / (radius * radius)) + (1.0 / diffusion[f] + 2.0))
        leading = [jnp.ones((8, PADDED), F32), diagonal[0]]
        trailing = [jnp.ones((8, PADDED), F32), diagonal[7]]
        for s in range(1, 8):
            leading.append(diagonal[s] * leading[s] - leading[s - 1])
            trailing.append(diagonal[7 - s] * trailing[s] - trailing[s - 1])
        share = 1.0 / leading[8]
        scaled = [value * share for value in leading]

        def entry(i, j):
            return scaled[min(i, j)] * trailing[7 - max(i, j)]

        for i in range(SLABS):
            for j in range(i, SLABS):
                inv[f, 0, i, j] = jnp.where(first_shell, entry(2 * i, 2 * j), entry(2 * i + 1, 2 * j + 1))
                inv[f, 1, i, j] = jnp.where(first_shell, entry(2 * i, 2 * j + 1), entry(2 * i + 1, 2 * j))
                if i != j:
                    inv[f, 0, j, i] = jnp.where(first_shell, entry(2 * i, 2 * j), entry(2 * i + 1, 2 * j + 1))
                    inv[f, 1, j, i] = jnp.where(first_shell, entry(2 * i + 1, 2 * j), entry(2 * i, 2 * j + 1))

    others = len(ALL_STEPS)
    pltpu.make_async_copy(r3.at[0:others], r3.at[0:others], sem_3r.at[0]).wait()

    mid4[...] = r3[...].astype(F32).reshape(512, 128)
    for g in range(3):
        flat[g * 128 : (g + 1) * 128, :] = jnp.concatenate(
            [mid4[pl.ds(y * 4 + g, FAR, stride=32), :] for y in range(NEAR)], axis=0
        ).T
    lhs = jnp.concatenate([flat[b * 96 : (b + 1) * 96, :] for b in range(4)], axis=1).astype(BF16)
    first_pair = lax.rem(lax.broadcasted_iota(jnp.int32, (96, PADDED), 0), 2) == 0
    nonlinear = jnp.where(first_pair, nt(lhs, masked[0]), nt(lhs, masked[1]))
    for f in range(3):
        own = st[f * 8 : (f + 1) * 8, :] * (2.0 / diffusion[f])
        drives, swapped = [], []
        for i in range(SLABS):
            start = f * 32 + i * 8
            mine = (slab == i).astype(F32)
            drive = nonlinear[start : start + 8] * coupling[f] + own * mine
            drives.append(drive)
            swapped.append(pltpu.roll(drive, 4, 0))
        for i in range(SLABS):
            value = inv[f, 0, i, 0] * drives[0] + inv[f, 1, i, 0] * swapped[0]
            for j in range(1, SLABS):
                value = value + inv[f, 0, i, j] * drives[j] + inv[f, 1, i, j] * swapped[j]
            send_x[i, f * 8 : (f + 1) * 8, :] = value
    last = [x_copy(send_x.at[x_peer(X_STEPS[i])], recv_x.at[i], i, sem_us, sem_ur) for i in range(SLABS - 1)]
    for copy in last:
        copy.start()
    total[...] = send_x[slab] - st[...]
    for copy in last:
        copy.wait_recv()
    total[...] = total[...] + recv_x[0] + recv_x[1] + recv_x[2]
    for f in range(3):
        for s in range(2):
            for c in range(2):
                for p in range(2):
                    row = f * 8 + s * 4 + c * 2 + p
                    out[p, f, s, c : c + 1, :] = total[row : row + 1, 0:ROWS]
    for copy in coefs + hop1 + hop2 + last:
        copy.wait_send()
    pltpu.make_async_copy(s3.at[0:others], s3.at[0:others], sem_3s.at[0]).wait()


def body(spectral_state, synthesis_table, low_orders, diffusion, coupling):
    low_row = low_orders.reshape(1, HALF)
    vmem = pl.BlockSpec(memory_space=pltpu.VMEM)
    hbm = pl.BlockSpec(memory_space=pltpu.HBM)
    dma = pltpu.SemaphoreType.DMA
    return pl.pallas_call(
        kernel,
        out_shape=pltpu.VMEM(spectral_state.shape, F32),
        in_specs=[hbm] * 7,
        out_specs=vmem,
        scratch_shapes=[
            pltpu.VMEM(spectral_state.shape, F32),
            pltpu.VMEM((ROWS, 2, 128), BF16),
            pltpu.VMEM((2 * ROWS, 128), F32),
            pltpu.VMEM((1, HALF), jnp.int32),
            pltpu.SMEM((HALF,), jnp.int32),
            pltpu.SMEM((3,), F32),
            pltpu.SMEM((3,), F32),
            pltpu.VMEM((8, QUARTER, HALF), BF16),
            pltpu.VMEM((8, QUARTER, HALF), BF16),
            pltpu.VMEM((2, PADDED, 512), BF16),
            pltpu.VMEM((24, PADDED), F32),
            pltpu.VMEM((SLABS, 24, PADDED), BF16),
            pltpu.VMEM((384, 128), F32),
            pltpu.VMEM((NEAR, FAR, 384), BF16),
            pltpu.VMEM((FAR, 24, 128), BF16),
            pltpu.VMEM((NEAR, FAR, 384), BF16),
            pltpu.VMEM((FAR, 24, 128), BF16),
            pltpu.VMEM((128, 4, 128), BF16),
            pltpu.VMEM((128, 4, 128), BF16),
            pltpu.VMEM((3, 128, 128), F32),
            pltpu.VMEM((512, 128), F32),
            pltpu.VMEM((3, 2, SLABS, SLABS, 8, PADDED), F32),
            pltpu.VMEM((SLABS, 24, PADDED), F32),
            pltpu.VMEM((SLABS - 1, 24, PADDED), F32),
            pltpu.VMEM((24, PADDED), F32),
            pltpu.SemaphoreType.REGULAR((2,)),
            dma((7,)),
            dma((SLABS - 1,)), dma((SLABS - 1,)),
            dma((NEAR - 1,)), dma((NEAR - 1,)),
            dma((FAR - 1,)), dma((FAR - 1,)),
            dma((1,)), dma((1,)),
            dma((SLABS - 1,)), dma((SLABS - 1,)),
        ],
        compiler_params=pltpu.CompilerParams(
            collective_id=0, has_side_effects=True, vmem_limit_bytes=63 * 1024 * 1024
        ),
    )(spectral_state, jnp.transpose(synthesis_table, (1, 0, 2)), low_row, low_orders, diffusion, coupling, jnp.asarray(wave_tables()))


def solution(mesh):
    placed = (P("mode", None, "radial", None, None), P("mode", None, "radial"), P(), P(), P())
    return jax.shard_map(
        body,
        mesh=mesh,
        in_specs=placed,
        out_specs=P("mode", None, "radial", None, None),
        check_vma=False,
    )
```
